32 devices in a mesh: ctx: 16 (over z, y, x), head: 2 (over core).
Axes of the slice: x: 2, y: 2, z: 4, core: 2. Of those that a mesh axis runs over, the one named last changes fastest.
Arguments:
- fresh_query: bfloat16 [256, 768], P('ctx', 'head'), may hold values from -64 to 64
- fresh_key: bfloat16 [256, 768], P('ctx', 'head'), may hold values from -2.5 to 2.5
- fresh_value: bfloat16 [256, 768], P('ctx', 'head'), may hold values from -6 to 6
- cache_key: bfloat16 [4096, 768], P('ctx', 'head'), may hold values from -6 to 6
- cache_value: bfloat16 [4096, 768], P('ctx', 'head'), may hold values from -6 to 6
- slot_owner: int32 [16], replicated, may hold values from 0 to 15, each once
- evictor: int32 [1], replicated, may hold values from 0 to 15
- timestep: int32 [1], replicated, may hold values from 0 to 49
- age_slope: float32 [6], P('head'), may hold values from 0.5 to 4
- time_gate: float32 [50, 768], P(None, 'head'), may hold values from 0.5 to 2
Outputs:
- attn_output: bfloat16 [256, 768], P('ctx', 'head')
- next_key: bfloat16 [4096, 768], P('ctx', 'head')
- next_value: bfloat16 [4096, 768], P('ctx', 'head')
The draws below stay inside these ranges and needn't reach their ends.
Inputs may be any that keep to these rules, and one draw needn't show every extreme that they name: `slot_owner`: a permutation of the 16 owners.
All inputs are finite; a program needn't handle non-finite values.
Results may differ from the reference program's by a relative error of at most 0.003.
Values may be sent and summed in bfloat16 or wider, within the bound.
A program may use at most 64 MiB of HBM per device.

```python
import math
import jax
import jax.numpy as jnp
from jax import lax

HEAD_DIM = 128
TIMESTEPS = 50
FRESH_DEV = 16
HEADS = 6
FRESH = 256
CACHE_DEV = 256
CACHED = 4096
N_CTX = 16


def fresh_base(key):
    return jnp.clip(jax.random.normal(key, (FRESH, HEADS * HEAD_DIM), jnp.float32), -2.5, 2.5)


def draw_fresh_query(key, part):
    key = jax.random.fold_in(key, 11)
    return jnp.clip(3.0 * jax.random.normal(key, (FRESH, HEADS * HEAD_DIM), jnp.float32), -12.0, 12.0).astype(jnp.bfloat16)


def draw_fresh_key(key, part):
    base = fresh_base(key)
    return base.astype(jnp.bfloat16)


def block_levels(key, shape, pieces, least, largest):
    gain, own = 1.0, jax.random.fold_in(key, 6)
    for axis_at, parts in pieces:
        steps = jnp.exp(jax.random.uniform(jax.random.fold_in(own, axis_at), (parts,), jnp.float32, least / len(pieces), largest / len(pieces)))
        gain = gain * jnp.repeat(steps, shape[axis_at] // parts).reshape([-1 if axis == axis_at else 1 for axis in range(len(shape))])
    return gain


def bell_draw(stream_key, dims, width, most, cuts=(), held_as=jnp.bfloat16):
    level = block_levels(stream_key, dims, cuts, -0.22, 0.18) if cuts else 1.0
    entries = jax.random.normal(stream_key, dims, jnp.float32) * width * level
    return jnp.minimum(jnp.maximum(entries, -most), most).astype(held_as)


def setup_inputs(seed: int = 0) -> dict:
    keys = jax.random.split(jax.random.key(seed), 11)
    return {
        "fresh_query": draw_fresh_query(jax.random.fold_in(keys[10], 71), 0),
        "fresh_key": draw_fresh_key(jax.random.fold_in(keys[10], 71), 0),
        "fresh_value": bell_draw(keys[2], (FRESH, HEADS * HEAD_DIM), 1.0, 6.0, ((0, 16), (1, 2))),
        "cache_key": bell_draw(keys[3], (CACHED, HEADS * HEAD_DIM), 1.0, 6.0, ((0, 16), (1, 2))),
        "cache_value": bell_draw(keys[4], (CACHED, HEADS * HEAD_DIM), 1.0, 6.0, ((0, 16), (1, 2))),
        "slot_owner": jax.random.permutation(keys[5], N_CTX).astype(jnp.int32),
        "evictor": jax.random.randint(keys[6], (1,), 0, N_CTX).astype(jnp.int32),
        "timestep": jax.random.randint(keys[7], (1,), 0, TIMESTEPS).astype(jnp.int32),
        "age_slope": jnp.clip(jnp.exp(math.log(4.0) - 2.0794415 * jax.random.uniform(keys[8], (HEADS,), jnp.float32) ** block_levels(keys[8], (HEADS,), ((0, 2),), -0.2, 0.2)), 0.5, 4.0),
        "time_gate": jnp.clip(0.5 + 1.5 * jax.random.uniform(keys[9], (TIMESTEPS, HEADS * HEAD_DIM), jnp.float32) ** block_levels(keys[9], (TIMESTEPS, HEADS * HEAD_DIM), ((1, 2),), -0.2, 0.2), 0.5, 2.0),
    }


def reference(fresh_query, fresh_key, fresh_value, cache_key, cache_value, slot_owner, evictor, timestep, age_slope, time_gate):
    owner_ids = jnp.arange(N_CTX, dtype=jnp.int32)
    slot_rank = lax.optimization_barrier(jnp.sum(jnp.where(slot_owner[None, :] == owner_ids[:, None], owner_ids[None, :], 0), axis=1))
    cache_age = (slot_rank + 1).astype(jnp.float32) / N_CTX
    key_age = jnp.concatenate([jnp.zeros((FRESH,), jnp.float32), jnp.repeat(cache_age, CACHE_DEV)])
    all_keys = jnp.concatenate([fresh_key, cache_key], 0).reshape(-1, HEADS, HEAD_DIM).transpose(1, 0, 2)
    all_values = jnp.concatenate([fresh_value, cache_value], 0).reshape(-1, HEADS, HEAD_DIM).transpose(1, 0, 2)
    queries = fresh_query.reshape(FRESH, HEADS, HEAD_DIM).transpose(1, 0, 2)
    score_scale = 1.0 / math.sqrt(HEAD_DIM)

    def group_terms(part_scores, group_max, part_values):
        rounded = lax.optimization_barrier(jnp.exp(part_scores - group_max[:, :, None]).astype(jnp.bfloat16))
        weights = rounded.astype(jnp.float32)
        den = lax.optimization_barrier(jnp.sum(weights, axis=2))
        num = jnp.einsum('ink,nkd->ind', weights, part_values, precision=lax.Precision.HIGHEST)
        return (num, den)

    def one_head(head_args):
        head_query, head_keys, head_values, slope = head_args
        scores = jnp.dot(head_query.astype(jnp.float32), head_keys.astype(jnp.float32).T, precision=lax.Precision.HIGHEST) * score_scale - slope * key_age[None, :]
        fresh_scores = scores[:, :FRESH].reshape(FRESH, N_CTX, FRESH_DEV)
        cache_scores = scores[:, FRESH:].reshape(FRESH, N_CTX, CACHE_DEV)
        values32 = head_values.astype(jnp.float32)
        fresh_vals = values32[:FRESH].reshape(N_CTX, FRESH_DEV, HEAD_DIM)
        cache_vals = values32[FRESH:].reshape(N_CTX, CACHE_DEV, HEAD_DIM)
        group_max = jnp.maximum(lax.optimization_barrier(jnp.max(fresh_scores, axis=2)), lax.optimization_barrier(jnp.max(cache_scores, axis=2)))
        num_a, den_a = group_terms(fresh_scores, group_max, fresh_vals)
        num_b, den_b = group_terms(cache_scores, group_max, cache_vals)
        row_max = lax.optimization_barrier(jnp.max(group_max, axis=1, keepdims=True))
        factor = jnp.exp(group_max - row_max)
        numerator = lax.optimization_barrier(jnp.sum(factor[:, :, None] * (num_a + num_b), axis=1))
        denominator = lax.optimization_barrier(jnp.sum(factor * (den_a + den_b), axis=1))
        return numerator / denominator[:, None]
    attended = lax.map(one_head, (queries, all_keys, all_values, age_slope))
    attended = attended.transpose(1, 0, 2).reshape(FRESH, HEADS * HEAD_DIM)
    squares = lax.optimization_barrier(jnp.sum(attended * attended, axis=1))
    inverse = lax.rsqrt(squares / (HEADS * HEAD_DIM) + 1e-06)
    gate_row = time_gate[timestep[0]]
    attn_output = (attended * inverse[:, None] * gate_row[None, :]).astype(jnp.bfloat16)
    start = (evictor[0] * CACHE_DEV).astype(jnp.int32)
    next_key = lax.dynamic_update_slice_in_dim(cache_key, fresh_key, start, 0)
    next_value = lax.dynamic_update_slice_in_dim(cache_value, fresh_value, start, 0)
    return (attn_output, next_key, next_value)
```

```python
import functools
import math

import jax
import jax.numpy as jnp
from jax import lax
from jax.experimental import pallas as pl
from jax.experimental.pallas import tpu as pltpu
from jax.sharding import PartitionSpec as P

MESH = pl.DeviceIdType.MESH
PLANES = 4
LANES = 128


def kernel(
    owners,
    head_devices,
    slot_ref,
    step_ref,
    slope_ref,
    query_in,
    key_in,
    value_in,
    cache_key_in,
    cache_value_in,
    gate_in,
    out_ref,
    all_keys,
    all_values,
    gath_key,
    gath_value,
    queries,
    keys,
    values,
    gate,
    sent,
    received,
    squares,
    local_sem,
    query_send,
    query_recv,
    part_send,
    part_recv,
    col_send,
    col_recv,
    plane_send,
    plane_recv,
    square_send,
    square_recv,
):
    rows, width = query_in.shape
    cache_rows = cache_key_in.shape[0]
    heads = slope_ref.shape[0]
    head_dim = width // heads
    plane = owners // PLANES
    me = lax.axis_index("ctx")
    my_head = lax.axis_index("head")
    my_z = me // plane
    my_p = lax.rem(me, plane)
    key_rows = keys.shape[0]

    barrier = pltpu.get_barrier_semaphore()

    def greet(step, carry):
        peer = lax.rem(me + step, owners)
        pl.semaphore_signal(barrier, inc=1, device_id=(peer, my_head), device_id_type=MESH)
        return carry

    lax.fori_loop(1, owners, greet, 0)
    for step in range(1, head_devices):
        peer = lax.rem(my_head + step, head_devices)
        pl.semaphore_signal(barrier, inc=1, device_id=(me, peer), device_id_type=MESH)

    locals_ = [
        pltpu.make_async_copy(query_in, queries.at[0], local_sem.at[0]),
        pltpu.make_async_copy(cache_key_in, keys.at[pl.ds(0, cache_rows)], local_sem.at[1]),
        pltpu.make_async_copy(key_in, keys.at[pl.ds(cache_rows, rows)], local_sem.at[2]),
        pltpu.make_async_copy(cache_value_in, values.at[pl.ds(0, cache_rows)], local_sem.at[3]),
        pltpu.make_async_copy(value_in, values.at[pl.ds(cache_rows, rows)], local_sem.at[4]),
        pltpu.make_async_copy(gate_in, gate, local_sem.at[5]),
        pltpu.make_async_copy(key_in, gath_key.at[0, 0], local_sem.at[6]),
        pltpu.make_async_copy(value_in, gath_value.at[0, 0], local_sem.at[7]),
    ]
    for copy in locals_:
        copy.start()
    spare = key_rows - cache_rows - rows
    keys[pl.ds(cache_rows + rows, spare), :] = jnp.zeros((spare, width), jnp.bfloat16)
    values[pl.ds(cache_rows + rows, spare), :] = jnp.zeros((spare, width), jnp.bfloat16)

    pl.semaphore_wait(barrier, owners - 1 + head_devices - 1)

    def device(dz, dp):
        z = lax.rem(my_z + dz + PLANES, PLANES)
        return (z * plane + lax.rem(my_p + dp + plane, plane), my_head)

    def query_copy(dz, dp):
        slot = dz * plane + dp
        return pltpu.make_async_remote_copy(
            src_ref=query_in,
            dst_ref=queries.at[slot],
            send_sem=query_send.at[slot],
            recv_sem=query_recv.at[slot],
            device_id=device(dz, dp),
            device_id_type=MESH,
        )

    def part_copy(dz, dp):
        slot = dz * plane + dp
        return pltpu.make_async_remote_copy(
            src_ref=sent.at[slot],
            dst_ref=received.at[slot],
            send_sem=part_send.at[slot],
            recv_sem=part_recv.at[slot],
            device_id=device(-dz, -dp),
            device_id_type=MESH,
        )

    def col_copy(kind, dz):
        return pltpu.make_async_remote_copy(
            src_ref=(key_in, value_in)[kind],
            dst_ref=(gath_key, gath_value)[kind].at[0, dz],
            send_sem=col_send.at[kind * PLANES + dz],
            recv_sem=col_recv.at[kind * PLANES + dz],
            device_id=device(dz, 0),
            device_id_type=MESH,
        )

    def plane_copy(kind, dp):
        gathered = (gath_key, gath_value)[kind]
        return pltpu.make_async_remote_copy(
            src_ref=gathered.at[0],
            dst_ref=gathered.at[dp],
            send_sem=plane_send.at[kind * plane + dp],
            recv_sem=plane_recv.at[kind * plane + dp],
            device_id=device(0, dp),
            device_id_type=MESH,
        )

    def peers(dz):
        return range(0 if dz else 1, plane)

    for dz in range(PLANES):
        for dp in peers(dz):
            query_copy(dz, dp).start()
    for dz in range(1, PLANES):
        for kind in range(2):
            col_copy(kind, dz).start()

    slot_rank = jnp.int32(0)
    for slot in range(owners):
        slot_rank += jnp.where(slot_ref[slot] == me, slot, 0)
    age = (slot_rank + 1).astype(jnp.float32) * (1.0 / owners)
    scale = 1.0 / math.sqrt(head_dim)
    tokens = plane * rows
    column = lax.broadcasted_iota(jnp.int32, (1, key_rows), 1)
    lane = lax.broadcasted_iota(jnp.int32, (tokens, LANES), 1)
    group, piece = lane >> 3, lane & 7
    ones = jnp.ones((key_rows, LANES), jnp.bfloat16)

    def weigh(dz):
        slots = slice(dz * plane, (dz + 1) * plane)
        query = queries[slots].reshape(tokens, width)
        stat = jnp.zeros((tokens, LANES), jnp.float32)
        for head in range(heads):
            cut = slice(head * head_dim, (head + 1) * head_dim)
            penalty = jnp.where(
                column < cache_rows,
                slope_ref[head] * age,
                jnp.where(column < cache_rows + rows, 0.0, 1e30),
            )
            scores = (
                lax.dot_general(
                    query[:, cut],
                    keys[:, cut],
                    (((1,), (1,)), ((), ())),
                    preferred_element_type=jnp.float32,
                )
                * scale
                - penalty
            )
            largest = jnp.max(scores, axis=1, keepdims=True)
            weights = jnp.exp(scores - largest).astype(jnp.bfloat16)
            both = jnp.dot(
                weights,
                jnp.concatenate([values[:, cut], ones], axis=1),
                preferred_element_type=jnp.float32,
            )
            numer, denom = both[:, :head_dim], both[:, head_dim:]
            sent[slots, :, cut] = numer.astype(jnp.bfloat16).reshape(plane, rows, head_dim)
            stat = jnp.where(group == head, jnp.where(piece < 3, largest, denom), stat)
        high = stat.astype(jnp.bfloat16).astype(jnp.float32)
        rest = stat - high
        middle = rest.astype(jnp.bfloat16).astype(jnp.float32)
        low = rest - middle
        third = jnp.where(piece < 3, piece, piece - 3)
        cuts = jnp.where(third == 0, high, jnp.where(third == 1, middle, low))
        sent[slots, :, width:] = cuts.astype(jnp.bfloat16).reshape(plane, rows, LANES)

    for copy in locals_:
        copy.wait()

    for dz in range(PLANES):
        for dp in peers(dz):
            query_copy(dz, dp).wait_recv()
        weigh(dz)
        for dp in peers(dz):
            part_copy(dz, dp).start()
    received[0] = sent[0]

    for kind in range(2):
        for dz in range(1, PLANES):
            col_copy(kind, dz).wait_recv()
        for dp in peers(0):
            plane_copy(kind, dp).start()

    for dz in range(PLANES):
        for dp in peers(dz):
            part_copy(dz, dp).wait_recv()

    stats = received[:, :, width:].astype(jnp.float32).reshape(owners * rows, LANES)
    stats = (
        stats
        + pltpu.roll(stats, LANES - 1, axis=1)
        + pltpu.roll(stats, LANES - 2, axis=1)
    )
    denoms = pltpu.roll(stats, LANES - 3, axis=1).reshape(owners, rows, LANES)
    maxima = stats.reshape(owners, rows, LANES)
    factor = jnp.exp(maxima - jnp.max(maxima, axis=0, keepdims=True))
    share = factor / jnp.sum(factor * denoms, axis=0, keepdims=True)
    attended = []
    for head in range(heads):
        cut = slice(head * head_dim, (head + 1) * head_dim)
        attended.append(
            jnp.sum(
                share[:, :, 8 * head : 8 * head + 1] * received[:, :, cut].astype(jnp.float32),
                axis=0,
            )
        )
    total = attended[0] * attended[0]
    for block in attended[1:]:
        total += block * block
    squares[0] = jnp.broadcast_to(jnp.sum(total, axis=1, keepdims=True), (rows, LANES))

    def square_copy(step):
        return pltpu.make_async_remote_copy(
            src_ref=squares.at[0],
            dst_ref=squares.at[step],
            send_sem=square_send.at[step],
            recv_sem=square_recv.at[step],
            device_id=(me, lax.rem(my_head + step, head_devices)),
            device_id_type=MESH,
        )

    for step in range(1, head_devices):
        square_copy(step).start()
    for dz in range(PLANES):
        for dp in peers(dz):
            query_copy(dz, dp).wait_send()
            part_copy(dz, dp).wait_send()
    moment = lax.broadcasted_iota(jnp.int32, gate.shape, 0) == step_ref[0]
    gate_row = jnp.sum(jnp.where(moment, gate[...], 0.0), axis=0, keepdims=True)
    for kind in range(2):
        for dz in range(1, PLANES):
            col_copy(kind, dz).wait_send()
        for dp in peers(0):
            plane_copy(kind, dp).wait_recv()
    for dz in range(PLANES):
        z = lax.rem(my_z - dz + PLANES, PLANES)
        for dp in range(plane):
            p = lax.rem(my_p - dp + plane, plane)
            all_keys[z, p] = gath_key[dp, dz]
            all_values[z, p] = gath_value[dp, dz]
    for step in range(1, head_devices):
        square_copy(step).wait_recv()
    mean = jnp.sum(squares[...], axis=0) * (1.0 / (width * head_devices))
    inverse = lax.rsqrt(mean + 1e-06)
    for head in range(heads):
        cut = slice(head * head_dim, (head + 1) * head_dim)
        out_ref[:, cut] = (attended[head] * inverse * gate_row[:, cut]).astype(jnp.bfloat16)

    for step in range(1, head_devices):
        square_copy(step).wait_send()
    for kind in range(2):
        for dp in peers(0):
            plane_copy(kind, dp).wait_send()


def body(
    fresh_query,
    fresh_key,
    fresh_value,
    cache_key,
    cache_value,
    slot_owner,
    evictor,
    timestep,
    age_slope,
    time_gate,
):
    rows, width = fresh_query.shape
    cache_rows = cache_key.shape[0]
    owners = lax.axis_size("ctx")
    head_devices = lax.axis_size("head")
    plane = owners // PLANES
    key_rows = cache_rows + LANES * pl.cdiv(rows, LANES)
    smem = pl.BlockSpec(memory_space=pltpu.SMEM)
    vmem = pl.BlockSpec(memory_space=pltpu.VMEM)
    anywhere = pl.BlockSpec(memory_space=pltpu.HBM)
    bf16 = jnp.bfloat16
    dma = pltpu.SemaphoreType.DMA
    gathered = jax.ShapeDtypeStruct((PLANES, plane, rows, width), bf16)
    attn_output, fresh_keys, fresh_values = pl.pallas_call(
        functools.partial(kernel, owners, head_devices),
        out_shape=(jax.ShapeDtypeStruct((rows, width), bf16), gathered, gathered),
        in_specs=[smem] * 3 + [anywhere] * 6,
        out_specs=(vmem, vmem, vmem),
        scratch_shapes=[
            pltpu.VMEM((plane, PLANES, rows, width), bf16),
            pltpu.VMEM((plane, PLANES, rows, width), bf16),
            pltpu.VMEM((owners, rows, width), bf16),
            pltpu.VMEM((key_rows, width), bf16),
            pltpu.VMEM((key_rows, width), bf16),
            pltpu.VMEM(time_gate.shape, jnp.float32),
            pltpu.VMEM((owners, rows, width + LANES), bf16),
            pltpu.VMEM((owners, rows, width + LANES), bf16),
            pltpu.VMEM((head_devices, rows, LANES), jnp.float32),
            dma((8,)),
            dma((owners,)),
            dma((owners,)),
            dma((owners,)),
            dma((owners,)),
            dma((2 * PLANES,)),
            dma((2 * PLANES,)),
            dma((2 * plane,)),
            dma((2 * plane,)),
            dma((head_devices,)),
            dma((head_devices,)),
        ],
        compiler_params=pltpu.CompilerParams(
            collective_id=0, has_side_effects=True, vmem_limit_bytes=60 * 1024 * 1024
        ),
        name="attend",
    )(
        slot_owner,
        timestep,
        age_slope,
        fresh_query,
        fresh_key,
        fresh_value,
        cache_key,
        cache_value,
        time_gate,
    )
    evicted = lax.axis_index("ctx") == evictor[0]

    def rolled(gathered, cache):
        return jnp.where(evicted, gathered.reshape(cache.shape), cache)

    next_key, next_value = rolled(fresh_keys, cache_key), rolled(fresh_values, cache_value)
    return (attn_output, next_key, next_value)


def solution(mesh):
    return jax.shard_map(
        body,
        mesh=mesh,
        in_specs=(
            P("ctx", "head"),
            P("ctx", "head"),
            P("ctx", "head"),
            P("ctx", "head"),
            P("ctx", "head"),
            P(),
            P(),
            P(),
            P("head"),
            P(None, "head"),
        ),
        out_specs=(P("ctx", "head"), P("ctx", "head"), P("ctx", "head")),
        check_vma=False,
    )
```

```python
import functools
import math

import jax
import jax.numpy as jnp
from jax import lax
from jax.experimental import pallas as pl
from jax.experimental.pallas import tpu as pltpu
from jax.sharding import PartitionSpec as P

MESH = pl.DeviceIdType.MESH
PLANES = 4
LANES = 128


def kernel(
    owners,
    head_devices,
    slot_ref,
    step_ref,
    slope_ref,
    query_in,
    key_in,
    value_in,
    cache_key_in,
    cache_value_in,
    gate_in,
    out_ref,
    keys_out,
    values_out,
    all_keys,
    all_values,
    gath_key,
    gath_value,
    queries,
    keys,
    values,
    gate,
    sent,
    received,
    squares,
    local_sem,
    query_send,
    query_recv,
    part_send,
    part_recv,
    col_send,
    col_recv,
    plane_send,
    plane_recv,
    square_send,
    square_recv,
):
    rows, width = query_in.shape
    cache_rows = cache_key_in.shape[0]
    heads = slope_ref.shape[0]
    head_dim = width // heads
    plane = owners // PLANES
    me = lax.axis_index("ctx")
    my_head = lax.axis_index("head")
    my_z = me // plane
    my_p = lax.rem(me, plane)
    key_rows = keys.shape[0]

    barrier = pltpu.get_barrier_semaphore()

    def greet(step, carry):
        peer = lax.rem(me + step, owners)
        pl.semaphore_signal(barrier, inc=1, device_id=(peer, my_head), device_id_type=MESH)
        return carry

    lax.fori_loop(1, owners, greet, 0)
    for step in range(1, head_devices):
        peer = lax.rem(my_head + step, head_devices)
        pl.semaphore_signal(barrier, inc=1, device_id=(me, peer), device_id_type=MESH)

    locals_ = [
        pltpu.make_async_copy(query_in, queries.at[0], local_sem.at[0]),
        pltpu.make_async_copy(cache_key_in, keys.at[pl.ds(0, cache_rows)], local_sem.at[1]),
        pltpu.make_async_copy(key_in, keys.at[pl.ds(cache_rows, rows)], local_sem.at[2]),
        pltpu.make_async_copy(cache_value_in, values.at[pl.ds(0, cache_rows)], local_sem.at[3]),
        pltpu.make_async_copy(value_in, values.at[pl.ds(cache_rows, rows)], local_sem.at[4]),
        pltpu.make_async_copy(gate_in, gate, local_sem.at[5]),
        pltpu.make_async_copy(key_in, gath_key.at[0, 0], local_sem.at[6]),
        pltpu.make_async_copy(value_in, gath_value.at[0, 0], local_sem.at[7]),
    ]
    for copy in locals_:
        copy.start()
    spare = key_rows - cache_rows - rows
    keys[pl.ds(cache_rows + rows, spare), :] = jnp.zeros((spare, width), jnp.bfloat16)
    values[pl.ds(cache_rows + rows, spare), :] = jnp.zeros((spare, width), jnp.bfloat16)

    pl.semaphore_wait(barrier, owners - 1 + head_devices - 1)

    def device(dz, dp):
        z = lax.rem(my_z + dz + PLANES, PLANES)
        return (z * plane + lax.rem(my_p + dp + plane, plane), my_head)

    def query_copy(dz, dp, relayed=False):
        slot = dp * PLANES + dz
        return pltpu.make_async_remote_copy(
            src_ref=queries.at[dz] if relayed else query_in,
            dst_ref=queries.at[slot],
            send_sem=query_send.at[slot],
            recv_sem=query_recv.at[slot],
            device_id=device(0 if relayed else dz, dp),
            device_id_type=MESH,
        )

    def part_copy(dz, dp):
        slot = dp * PLANES + dz
        return pltpu.make_async_remote_copy(
            src_ref=sent.at[slot],
            dst_ref=received.at[slot],
            send_sem=part_send.at[slot],
            recv_sem=part_recv.at[slot],
            device_id=device(-dz, -dp),
            device_id_type=MESH,
        )

    def col_copy(kind, dz):
        return pltpu.make_async_remote_copy(
            src_ref=(key_in, value_in)[kind],
            dst_ref=(gath_key, gath_value)[kind].at[0, dz],
            send_sem=col_send.at[kind * PLANES + dz],
            recv_sem=col_recv.at[kind * PLANES + dz],
            device_id=device(dz, 0),
            device_id_type=MESH,
        )

    def plane_copy(kind, dp):
        gathered = (gath_key, gath_value)[kind]
        return pltpu.make_async_remote_copy(
            src_ref=gathered.at[0],
            dst_ref=gathered.at[dp],
            send_sem=plane_send.at[kind * plane + dp],
            recv_sem=plane_recv.at[kind * plane + dp],
            device_id=device(0, dp),
            device_id_type=MESH,
        )

    others = [(dz, dp) for dp in range(plane) for dz in range(PLANES) if dz or dp]

    for dz in range(1, PLANES):
        query_copy(dz, 0).start()
    for dp in range(1, plane):
        query_copy(0, dp).start()
    for dz in range(1, PLANES):
        for kind in range(2):
            col_copy(kind, dz).start()

    slot_rank = jnp.int32(0)
    for slot in range(owners):
        slot_rank += jnp.where(slot_ref[slot] == me, slot, 0)
    age = (slot_rank + 1).astype(jnp.float32) * (1.0 / owners)
    scale = 1.0 / math.sqrt(head_dim)
    tokens = PLANES * rows
    column = lax.broadcasted_iota(jnp.int32, (1, key_rows), 1)
    lane = lax.broadcasted_iota(jnp.int32, (tokens, LANES), 1)
    group, piece = lane >> 3, lane & 7
    ones = jnp.ones((key_rows, LANES), jnp.bfloat16)

    def weigh(dp):
        slots = slice(dp * PLANES, (dp + 1) * PLANES)
        query = queries[slots].reshape(tokens, width)
        stat = jnp.zeros((tokens, LANES), jnp.float32)
        for head in range(heads):
            cut = slice(head * head_dim, (head + 1) * head_dim)
            penalty = jnp.where(
                column < cache_rows,
                slope_ref[head] * age,
                jnp.where(column < cache_rows + rows, 0.0, 1e30),
            )
            scores = (
                lax.dot_general(
                    query[:, cut],
                    keys[:, cut],
                    (((1,), (1,)), ((), ())),
                    preferred_element_type=jnp.float32,
                )
                * scale
                - penalty
            )
            largest = jnp.max(scores, axis=1, keepdims=True)
            weights = jnp.exp(scores - largest).astype(jnp.bfloat16)
            both = jnp.dot(
                weights,
                jnp.concatenate([values[:, cut], ones], axis=1),
                preferred_element_type=jnp.float32,
            )
            numer, denom = both[:, :head_dim], both[:, head_dim:]
            sent[slots, :, cut] = numer.astype(jnp.bfloat16).reshape(PLANES, rows, head_dim)
            stat = jnp.where(group == head, jnp.where(piece < 3, largest, denom), stat)
        high = stat.astype(jnp.bfloat16).astype(jnp.float32)
        rest = stat - high
        middle = rest.astype(jnp.bfloat16).astype(jnp.float32)
        low = rest - middle
        third = jnp.where(piece < 3, piece, piece - 3)
        cuts = jnp.where(third == 0, high, jnp.where(third == 1, middle, low))
        sent[slots, :, width:] = cuts.astype(jnp.bfloat16).reshape(PLANES, rows, LANES)

    for dz in range(1, PLANES):
        query_copy(dz, 0).wait_recv()
        for dp in range(1, plane):
            query_copy(dz, dp, relayed=True).start()
    for copy in locals_:
        copy.wait()

    for dp in range(plane):
        if dp:
            for dz in range(PLANES):
                query_copy(dz, dp).wait_recv()
        weigh(dp)
        for dz in range(0 if dp else 1, PLANES):
            part_copy(dz, dp).start()
    received[0] = sent[0]

    for kind in range(2):
        for dz in range(1, PLANES):
            col_copy(kind, dz).wait_recv()
        for dp in range(1, plane):
            plane_copy(kind, dp).start()

    for dz, dp in others:
        part_copy(dz, dp).wait_recv()

    stats = received[:, :, width:].astype(jnp.float32).reshape(owners * rows, LANES)
    stats = (
        stats
        + pltpu.roll(stats, LANES - 1, axis=1)
        + pltpu.roll(stats, LANES - 2, axis=1)
    )
    denoms = pltpu.roll(stats, LANES - 3, axis=1).reshape(owners, rows, LANES)
    maxima = stats.reshape(owners, rows, LANES)
    factor = jnp.exp(maxima - jnp.max(maxima, axis=0, keepdims=True))
    share = factor / jnp.sum(factor * denoms, axis=0, keepdims=True)
    attended = []
    for head in range(heads):
        cut = slice(head * head_dim, (head + 1) * head_dim)
        attended.append(
            jnp.sum(
                share[:, :, 8 * head : 8 * head + 1] * received[:, :, cut].astype(jnp.float32),
                axis=0,
            )
        )
    total = attended[0] * attended[0]
    for block in attended[1:]:
        total += block * block
    squares[0] = jnp.broadcast_to(jnp.sum(total, axis=1, keepdims=True), (rows, LANES))

    def square_copy(step):
        return pltpu.make_async_remote_copy(
            src_ref=squares.at[0],
            dst_ref=squares.at[step],
            send_sem=square_send.at[step],
            recv_sem=square_recv.at[step],
            device_id=(me, lax.rem(my_head + step, head_devices)),
            device_id_type=MESH,
        )

    for step in range(1, head_devices):
        square_copy(step).start()
    for dz, dp in others:
        query_copy(dz, dp).wait_send()
        part_copy(dz, dp).wait_send()
    moment = lax.broadcasted_iota(jnp.int32, gate.shape, 0) == step_ref[0]
    gate_row = jnp.sum(jnp.where(moment, gate[...], 0.0), axis=0, keepdims=True)
    for kind in range(2):
        for dz in range(1, PLANES):
            col_copy(kind, dz).wait_send()
        for dp in range(1, plane):
            plane_copy(kind, dp).wait_recv()
    for dz in range(PLANES):
        z = lax.rem(my_z - dz + PLANES, PLANES)
        for dp in range(plane):
            p = lax.rem(my_p - dp + plane, plane)
            all_keys[z, p] = gath_key[dp, dz]
            all_values[z, p] = gath_value[dp, dz]
    handed = [
        pltpu.make_async_copy(all_keys, keys_out, local_sem.at[0]),
        pltpu.make_async_copy(all_values, values_out, local_sem.at[1]),
    ]
    for copy in handed:
        copy.start()
    for step in range(1, head_devices):
        square_copy(step).wait_recv()
    mean = jnp.sum(squares[...], axis=0) * (1.0 / (width * head_devices))
    inverse = lax.rsqrt(mean + 1e-06)
    for head in range(heads):
        cut = slice(head * head_dim, (head + 1) * head_dim)
        out_ref[:, cut] = (attended[head] * inverse * gate_row[:, cut]).astype(jnp.bfloat16)

    for step in range(1, head_devices):
        square_copy(step).wait_send()
    for kind in range(2):
        for dp in range(1, plane):
            plane_copy(kind, dp).wait_send()
    for copy in handed:
        copy.wait()


def finish(
    evictor_ref,
    attended_in,
    all_keys,
    all_values,
    cache_key_in,
    cache_value_in,
    out_ref,
    next_key,
    next_value,
    sem,
):
    output = pltpu.make_async_copy(attended_in, out_ref, sem.at[0])
    output.start()

    def roll(key_from, value_from):
        moves = [
            pltpu.make_async_copy(key_from, next_key, sem.at[1]),
            pltpu.make_async_copy(value_from, next_value, sem.at[2]),
        ]
        for move in moves:
            move.start()
        for move in moves:
            move.wait()

    evicted = lax.axis_index("ctx") == evictor_ref[0]
    pl.when(evicted)(lambda: roll(all_keys, all_values))
    pl.when(jnp.logical_not(evicted))(lambda: roll(cache_key_in, cache_value_in))
    output.wait()


def body(
    fresh_query,
    fresh_key,
    fresh_value,
    cache_key,
    cache_value,
    slot_owner,
    evictor,
    timestep,
    age_slope,
    time_gate,
):
    rows, width = fresh_query.shape
    cache_rows = cache_key.shape[0]
    owners = lax.axis_size("ctx")
    head_devices = lax.axis_size("head")
    plane = owners // PLANES
    key_rows = cache_rows + LANES * pl.cdiv(rows, LANES)
    smem = pl.BlockSpec(memory_space=pltpu.SMEM)
    vmem = pl.BlockSpec(memory_space=pltpu.VMEM)
    anywhere = pl.BlockSpec(memory_space=pltpu.HBM)
    bf16 = jnp.bfloat16
    dma = pltpu.SemaphoreType.DMA
    gathered = jax.ShapeDtypeStruct((PLANES, plane, rows, width), bf16)
    attn_output, fresh_keys, fresh_values = pl.pallas_call(
        functools.partial(kernel, owners, head_devices),
        out_shape=(jax.ShapeDtypeStruct((rows, width), bf16), gathered, gathered),
        in_specs=[smem] * 3 + [anywhere] * 6,
        out_specs=(vmem, anywhere, anywhere),
        scratch_shapes=[
            pltpu.VMEM(gathered.shape, bf16),
            pltpu.VMEM(gathered.shape, bf16),
            pltpu.VMEM((plane, PLANES, rows, width), bf16),
            pltpu.VMEM((plane, PLANES, rows, width), bf16),
            pltpu.VMEM((owners, rows, width), bf16),
            pltpu.VMEM((key_rows, width), bf16),
            pltpu.VMEM((key_rows, width), bf16),
            pltpu.VMEM(time_gate.shape, jnp.float32),
            pltpu.VMEM((owners, rows, width + LANES), bf16),
            pltpu.VMEM((owners, rows, width + LANES), bf16),
            pltpu.VMEM((head_devices, rows, LANES), jnp.float32),
            dma((8,)),
            dma((owners,)),
            dma((owners,)),
            dma((owners,)),
            dma((owners,)),
            dma((2 * PLANES,)),
            dma((2 * PLANES,)),
            dma((2 * plane,)),
            dma((2 * plane,)),
            dma((head_devices,)),
            dma((head_devices,)),
        ],
        compiler_params=pltpu.CompilerParams(
            collective_id=0, has_side_effects=True, vmem_limit_bytes=60 * 1024 * 1024
        ),
        name="attend",
    )(
        slot_owner,
        timestep,
        age_slope,
        fresh_query,
        fresh_key,
        fresh_value,
        cache_key,
        cache_value,
        time_gate,
    )
    cache_shape = jax.ShapeDtypeStruct(cache_key.shape, bf16)
    return pl.pallas_call(
        finish,
        out_shape=(jax.ShapeDtypeStruct((rows, width), bf16), cache_shape, cache_shape),
        in_specs=[smem] + [anywhere] * 5,
        out_specs=(anywhere, anywhere, anywhere),
        scratch_shapes=[dma((3,))],
        compiler_params=pltpu.CompilerParams(vmem_limit_bytes=60 * 1024 * 1024),
        name="finish",
    )(
        evictor,
        attn_output,
        fresh_keys.reshape(cache_key.shape),
        fresh_values.reshape(cache_value.shape),
        cache_key,
        cache_value,
    )


def solution(mesh):
    return jax.shard_map(
        body,
        mesh=mesh,
        in_specs=(
            P("ctx", "head"),
            P("ctx", "head"),
            P("ctx", "head"),
            P("ctx", "head"),
            P("ctx", "head"),
            P(),
            P(),
            P(),
            P("head"),
            P(None, "head"),
        ),
        out_specs=(P("ctx", "head"), P("ctx", "head"), P("ctx", "head")),
        check_vma=False,
    )
```

```python
import functools
import math

import jax
import jax.numpy as jnp
from jax import lax
from jax.experimental import pallas as pl
from jax.experimental.pallas import tpu as pltpu
from jax.sharding import PartitionSpec as P

MESH = pl.DeviceIdType.MESH
PLANES = 4
LANES = 128


def kernel(
    owners,
    head_devices,
    slot_in,
    step_in,
    slope_in,
    query_in,
    key_in,
    value_in,
    cache_key_in,
    cache_value_in,
    gate_in,
    out_ref,
    keys_out,
    values_out,
    all_keys,
    all_values,
    gath_key,
    gath_value,
    queries,
    keys,
    values,
    gate,
    sent,
    received,
    squares,
    slot_ref,
    step_ref,
    slope_ref,
    flat_keys,
    wide_values,
    local_sem,
    query_send,
    query_recv,
    part_send,
    part_recv,
    col_send,
    col_recv,
    plane_send,
    plane_recv,
    square_send,
    square_recv,
):
    rows, width = query_in.shape
    cache_rows = cache_key_in.shape[0]
    heads = slope_ref.shape[0]
    head_dim = width // heads
    plane = owners // PLANES
    me = lax.axis_index("ctx")
    my_head = lax.axis_index("head")
    my_z = me // plane
    my_p = lax.rem(me, plane)
    key_rows = keys.shape[0]

    barrier = pltpu.get_barrier_semaphore()

    def greet(step, carry):
        peer = lax.rem(me + step, owners)
        pl.semaphore_signal(barrier, inc=1, device_id=(peer, my_head), device_id_type=MESH)
        return carry

    lax.fori_loop(1, owners, greet, 0)
    for step in range(1, head_devices):
        peer = lax.rem(my_head + step, head_devices)
        pl.semaphore_signal(barrier, inc=1, device_id=(me, peer), device_id_type=MESH)

    locals_ = [
        pltpu.make_async_copy(query_in, queries.at[0], local_sem.at[0]),
        pltpu.make_async_copy(cache_key_in, keys.at[pl.ds(0, cache_rows)], local_sem.at[1]),
        pltpu.make_async_copy(key_in, keys.at[pl.ds(cache_rows, rows)], local_sem.at[2]),
        pltpu.make_async_copy(cache_value_in, values.at[pl.ds(0, cache_rows)], local_sem.at[3]),
        pltpu.make_async_copy(value_in, values.at[pl.ds(cache_rows, rows)], local_sem.at[4]),
        pltpu.make_async_copy(gate_in, gate, local_sem.at[5]),
        pltpu.make_async_copy(key_in, gath_key.at[0, 0], local_sem.at[6]),
        pltpu.make_async_copy(value_in, gath_value.at[0, 0], local_sem.at[7]),
        pltpu.make_async_copy(slot_in, slot_ref, local_sem.at[8]),
        pltpu.make_async_copy(step_in, step_ref, local_sem.at[9]),
        pltpu.make_async_copy(slope_in, slope_ref, local_sem.at[10]),
    ]
    for copy in locals_:
        copy.start()
    spare = key_rows - cache_rows - rows
    keys[pl.ds(cache_rows + rows, spare), :] = jnp.zeros((spare, width), jnp.bfloat16)
    values[pl.ds(cache_rows + rows, spare), :] = jnp.zeros((spare, width), jnp.bfloat16)

    pl.semaphore_wait(barrier, owners - 1 + head_devices - 1)

    def device(dz, dp):
        z = lax.rem(my_z + dz + PLANES, PLANES)
        return (z * plane + lax.rem(my_p + dp + plane, plane), my_head)

    def query_copy(dz, dp, relayed=False):
        slot = dp * PLANES + dz
        return pltpu.make_async_remote_copy(
            src_ref=queries.at[dz] if relayed else query_in,
            dst_ref=queries.at[slot],
            send_sem=query_send.at[slot],
            recv_sem=query_recv.at[slot],
            device_id=device(0 if relayed else dz, dp),
            device_id_type=MESH,
        )

    def part_copy(dz, dp):
        slot = dp * PLANES + dz
        return pltpu.make_async_remote_copy(
            src_ref=sent.at[slot],
            dst_ref=received.at[slot],
            send_sem=part_send.at[slot],
            recv_sem=part_recv.at[slot],
            device_id=device(-dz, -dp),
            device_id_type=MESH,
        )

    def col_copy(kind, dz):
        return pltpu.make_async_remote_copy(
            src_ref=(key_in, value_in)[kind],
            dst_ref=(gath_key, gath_value)[kind].at[0, dz],
            send_sem=col_send.at[kind * PLANES + dz],
            recv_sem=col_recv.at[kind * PLANES + dz],
            device_id=device(dz, 0),
            device_id_type=MESH,
        )

    def plane_copy(kind, dp):
        gathered = (gath_key, gath_value)[kind]
        return pltpu.make_async_remote_copy(
            src_ref=gathered.at[0],
            dst_ref=gathered.at[dp],
            send_sem=plane_send.at[kind * plane + dp],
            recv_sem=plane_recv.at[kind * plane + dp],
            device_id=device(0, dp),
            device_id_type=MESH,
        )

    others = [(dz, dp) for dp in range(plane) for dz in range(PLANES) if dz or dp]

    for dz in range(1, PLANES):
        query_copy(dz, 0).start()
    for dp in range(1, plane):
        query_copy(0, dp).start()
    for dz in range(1, PLANES):
        for kind in range(2):
            col_copy(kind, dz).start()

    for copy in locals_:
        copy.wait()
    slot_rank = jnp.int32(0)
    for slot in range(owners):
        slot_rank += jnp.where(slot_ref[slot] == me, slot, 0)
    age = (slot_rank + 1).astype(jnp.float32) * (1.0 / owners)
    scale = 1.0 / math.sqrt(head_dim)
    tokens = PLANES * rows
    column = lax.broadcasted_iota(jnp.int32, (1, key_rows), 1)
    lane = lax.broadcasted_iota(jnp.int32, (tokens, LANES), 1)
    group, piece = lane >> 3, lane & 7
    for head in range(heads):
        cut = slice(head * head_dim, (head + 1) * head_dim)
        flat_keys[cut, :] = keys[:, cut].T
        wide_values[head, :, :head_dim] = values[:, cut]
        wide_values[head, :, head_dim:] = jnp.ones((key_rows, LANES), jnp.bfloat16)

    def weigh(dp):
        slots = slice(dp * PLANES, (dp + 1) * PLANES)
        query = queries[slots].reshape(tokens, width)
        stat = jnp.zeros((tokens, LANES), jnp.float32)
        for head in range(heads):
            cut = slice(head * head_dim, (head + 1) * head_dim)
            penalty = jnp.where(
                column < cache_rows,
                slope_ref[head] * age,
                jnp.where(column < cache_rows + rows, 0.0, 1e30),
            )
            scores = (
                jnp.dot(query[:, cut], flat_keys[cut, :], preferred_element_type=jnp.float32)
                * scale
                - penalty
            )
            largest = jnp.max(scores, axis=1, keepdims=True)
            weights = jnp.exp(scores - largest).astype(jnp.bfloat16)
            both = jnp.dot(weights, wide_values[head], preferred_element_type=jnp.float32)
            numer, denom = both[:, :head_dim], both[:, head_dim:]
            sent[slots, :, cut] = numer.astype(jnp.bfloat16).reshape(PLANES, rows, head_dim)
            stat = jnp.where(group == head, jnp.where(piece < 3, largest, denom), stat)
        high = stat.astype(jnp.bfloat16).astype(jnp.float32)
        rest = stat - high
        middle = rest.astype(jnp.bfloat16).astype(jnp.float32)
        low = rest - middle
        third = jnp.where(piece < 3, piece, piece - 3)
        cuts = jnp.where(third == 0, high, jnp.where(third == 1, middle, low))
        sent[slots, :, width:] = cuts.astype(jnp.bfloat16).reshape(PLANES, rows, LANES)

    for dz in range(1, PLANES):
        query_copy(dz, 0).wait_recv()
        for dp in range(1, plane):
            query_copy(dz, dp, relayed=True).start()

    for dp in range(plane):
        if dp:
            for dz in range(PLANES):
                query_copy(dz, dp).wait_recv()
        weigh(dp)
        for dz in range(0 if dp else 1, PLANES):
            part_copy(dz, dp).start()
    received[0] = sent[0]

    for kind in range(2):
        for dz in range(1, PLANES):
            col_copy(kind, dz).wait_recv()
        for dp in range(1, plane):
            plane_copy(kind, dp).start()

    for dz, dp in others:
        part_copy(dz, dp).wait_recv()

    stats = received[:, :, width:].astype(jnp.float32).reshape(owners * rows, LANES)
    stats = (
        stats
        + pltpu.roll(stats, LANES - 1, axis=1)
        + pltpu.roll(stats, LANES - 2, axis=1)
    )
    denoms = pltpu.roll(stats, LANES - 3, axis=1).reshape(owners, rows, LANES)
    maxima = stats.reshape(owners, rows, LANES)
    factor = jnp.exp(maxima - jnp.max(maxima, axis=0, keepdims=True))
    share = factor / jnp.sum(factor * denoms, axis=0, keepdims=True)
    attended = []
    for head in range(heads):
        cut = slice(head * head_dim, (head + 1) * head_dim)
        attended.append(
            jnp.sum(
                share[:, :, 8 * head : 8 * head + 1] * received[:, :, cut].astype(jnp.float32),
                axis=0,
            )
        )
    total = attended[0] * attended[0]
    for block in attended[1:]:
        total += block * block
    squares[0] = jnp.broadcast_to(jnp.sum(total, axis=1, keepdims=True), (rows, LANES))

    def square_copy(step):
        return pltpu.make_async_remote_copy(
            src_ref=squares.at[0],
            dst_ref=squares.at[step],
            send_sem=square_send.at[step],
            recv_sem=square_recv.at[step],
            device_id=(me, lax.rem(my_head + step, head_devices)),
            device_id_type=MESH,
        )

    for step in range(1, head_devices):
        square_copy(step).start()
    for dz, dp in others:
        query_copy(dz, dp).wait_send()
        part_copy(dz, dp).wait_send()
    moment = lax.broadcasted_iota(jnp.int32, gate.shape, 0) == step_ref[0]
    gate_row = jnp.sum(jnp.where(moment, gate[...], 0.0), axis=0, keepdims=True)
    for kind in range(2):
        for dz in range(1, PLANES):
            col_copy(kind, dz).wait_send()
        for dp in range(1, plane):
            plane_copy(kind, dp).wait_recv()
    for dz in range(PLANES):
        z = lax.rem(my_z - dz + PLANES, PLANES)
        for dp in range(plane):
            p = lax.rem(my_p - dp + plane, plane)
            all_keys[z, p] = gath_key[dp, dz]
            all_values[z, p] = gath_value[dp, dz]
    handed = [
        pltpu.make_async_copy(all_keys, keys_out, local_sem.at[0]),
        pltpu.make_async_copy(all_values, values_out, local_sem.at[1]),
    ]
    for copy in handed:
        copy.start()
    for step in range(1, head_devices):
        square_copy(step).wait_recv()
    mean = jnp.sum(squares[...], axis=0) * (1.0 / (width * head_devices))
    inverse = lax.rsqrt(mean + 1e-06)
    for head in range(heads):
        cut = slice(head * head_dim, (head + 1) * head_dim)
        out_ref[:, cut] = (attended[head] * inverse * gate_row[:, cut]).astype(jnp.bfloat16)

    for step in range(1, head_devices):
        square_copy(step).wait_send()
    for kind in range(2):
        for dp in range(1, plane):
            plane_copy(kind, dp).wait_send()
    for copy in handed:
        copy.wait()


def finish(
    evictor_ref,
    attended_in,
    all_keys,
    all_values,
    cache_key_in,
    cache_value_in,
    out_ref,
    next_key,
    next_value,
    attended,
    held,
    sem,
):
    first = pltpu.make_async_copy(attended_in, attended, sem.at[0])
    first.start()

    def roll(key_from, value_from):
        loads = [
            pltpu.make_async_copy(key_from, held.at[0], sem.at[1]),
            pltpu.make_async_copy(value_from, held.at[1], sem.at[2]),
        ]
        stores = [
            pltpu.make_async_copy(held.at[0], next_key, sem.at[1]),
            pltpu.make_async_copy(held.at[1], next_value, sem.at[2]),
        ]
        output = pltpu.make_async_copy(attended, out_ref, sem.at[0])
        for load in loads:
            load.start()
        first.wait()
        output.start()
        for load, store in zip(loads, stores):
            load.wait()
            store.start()
        output.wait()
        for store in stores:
            store.wait()

    evicted = lax.axis_index("ctx") == evictor_ref[0]
    pl.when(evicted)(lambda: roll(all_keys, all_values))
    pl.when(jnp.logical_not(evicted))(lambda: roll(cache_key_in, cache_value_in))


def body(
    fresh_query,
    fresh_key,
    fresh_value,
    cache_key,
    cache_value,
    slot_owner,
    evictor,
    timestep,
    age_slope,
    time_gate,
):
    rows, width = fresh_query.shape
    cache_rows = cache_key.shape[0]
    owners = lax.axis_size("ctx")
    head_devices = lax.axis_size("head")
    plane = owners // PLANES
    heads = age_slope.shape[0]
    key_rows = cache_rows + LANES * pl.cdiv(rows, LANES)
    smem = pl.BlockSpec(memory_space=pltpu.SMEM)
    vmem = pl.BlockSpec(memory_space=pltpu.VMEM)
    anywhere = pl.BlockSpec(memory_space=pltpu.HBM)
    bf16 = jnp.bfloat16
    dma = pltpu.SemaphoreType.DMA
    gathered = jax.ShapeDtypeStruct((PLANES, plane, rows, width), bf16)
    attn_output, fresh_keys, fresh_values = pl.pallas_call(
        functools.partial(kernel, owners, head_devices),
        out_shape=(jax.ShapeDtypeStruct((rows, width), bf16), gathered, gathered),
        in_specs=[anywhere] * 9,
        out_specs=(vmem, anywhere, anywhere),
        scratch_shapes=[
            pltpu.VMEM(gathered.shape, bf16),
            pltpu.VMEM(gathered.shape, bf16),
            pltpu.VMEM((plane, PLANES, rows, width), bf16),
            pltpu.VMEM((plane, PLANES, rows, width), bf16),
            pltpu.VMEM((owners, rows, width), bf16),
            pltpu.VMEM((key_rows, width), bf16),
            pltpu.VMEM((key_rows, width), bf16),
            pltpu.VMEM(time_gate.shape, jnp.float32),
            pltpu.VMEM((owners, rows, width + LANES), bf16),
            pltpu.VMEM((owners, rows, width + LANES), bf16),
            pltpu.VMEM((head_devices, rows, LANES), jnp.float32),
            pltpu.SMEM(slot_owner.shape, jnp.int32),
            pltpu.SMEM(timestep.shape, jnp.int32),
            pltpu.SMEM(age_slope.shape, jnp.float32),
            pltpu.VMEM((width, key_rows), bf16),
            pltpu.VMEM((heads, key_rows, width // heads + LANES), bf16),
            dma((11,)),
            dma((owners,)),
            dma((owners,)),
            dma((owners,)),
            dma((owners,)),
            dma((2 * PLANES,)),
            dma((2 * PLANES,)),
            dma((2 * plane,)),
            dma((2 * plane,)),
            dma((head_devices,)),
            dma((head_devices,)),
        ],
        compiler_params=pltpu.CompilerParams(
            collective_id=0, has_side_effects=True, vmem_limit_bytes=60 * 1024 * 1024
        ),
        name="attend",
    )(
        slot_owner,
        timestep,
        age_slope,
        fresh_query,
        fresh_key,
        fresh_value,
        cache_key,
        cache_value,
        time_gate,
    )
    cache_shape = jax.ShapeDtypeStruct(cache_key.shape, bf16)
    return pl.pallas_call(
        finish,
        out_shape=(jax.ShapeDtypeStruct((rows, width), bf16), cache_shape, cache_shape),
        in_specs=[smem] + [anywhere] * 5,
        out_specs=(anywhere, anywhere, anywhere),
        scratch_shapes=[
            pltpu.VMEM((rows, width), bf16),
            pltpu.VMEM((2,) + cache_key.shape, bf16),
            dma((3,)),
        ],
        compiler_params=pltpu.CompilerParams(vmem_limit_bytes=60 * 1024 * 1024),
        name="finish",
    )(
        evictor,
        attn_output,
        fresh_keys.reshape(cache_key.shape),
        fresh_values.reshape(cache_value.shape),
        cache_key,
        cache_value,
    )


def solution(mesh):
    return jax.shard_map(
        body,
        mesh=mesh,
        in_specs=(
            P("ctx", "head"),
            P("ctx", "head"),
            P("ctx", "head"),
            P("ctx", "head"),
            P("ctx", "head"),
            P(),
            P(),
            P(),
            P("head"),
            P(None, "head"),
        ),
        out_specs=(P("ctx", "head"), P("ctx", "head"), P("ctx", "head")),
        check_vma=False,
    )
```

```python
import functools
import math

import jax
import jax.numpy as jnp
from jax import lax
from jax.experimental import pallas as pl
from jax.experimental.pallas import tpu as pltpu
from jax.sharding import PartitionSpec as P

MESH = pl.DeviceIdType.MESH
PLANES = 4
LANES = 128


def kernel(
    owners,
    head_devices,
    slot_in,
    step_in,
    slope_in,
    query_in,
    key_in,
    value_in,
    cache_key_in,
    cache_value_in,
    gate_in,
    out_ref,
    keys_out,
    values_out,
    all_keys,
    all_values,
    gathered,
    queries,
    keys,
    values,
    gate,
    sent,
    received,
    squares,
    slot_ref,
    step_ref,
    slope_ref,
    flat_keys,
    wide_values,
    local_sem,
    query_send,
    query_recv,
    part_send,
    part_recv,
    col_send,
    col_recv,
    plane_send,
    plane_recv,
    square_send,
    square_recv,
):
    rows, width = query_in.shape
    cache_rows = cache_key_in.shape[0]
    heads = slope_ref.shape[0]
    head_dim = width // heads
    plane = owners // PLANES
    me = lax.axis_index("ctx")
    my_head = lax.axis_index("head")
    my_z = me // plane
    my_p = lax.rem(me, plane)
    key_rows = keys.shape[0]

    barrier = pltpu.get_barrier_semaphore()

    def greet(step, carry):
        peer = lax.rem(me + step, owners)
        pl.semaphore_signal(barrier, inc=1, device_id=(peer, my_head), device_id_type=MESH)
        return carry

    lax.fori_loop(1, owners, greet, 0)
    for step in range(1, head_devices):
        peer = lax.rem(my_head + step, head_devices)
        pl.semaphore_signal(barrier, inc=1, device_id=(me, peer), device_id_type=MESH)

    locals_ = [
        pltpu.make_async_copy(query_in, queries.at[0], local_sem.at[0]),
        pltpu.make_async_copy(cache_key_in, keys.at[pl.ds(0, cache_rows)], local_sem.at[1]),
        pltpu.make_async_copy(key_in, keys.at[pl.ds(cache_rows, rows)], local_sem.at[2]),
        pltpu.make_async_copy(cache_value_in, values.at[pl.ds(0, cache_rows)], local_sem.at[3]),
        pltpu.make_async_copy(value_in, values.at[pl.ds(cache_rows, rows)], local_sem.at[4]),
        pltpu.make_async_copy(gate_in, gate, local_sem.at[5]),
        pltpu.make_async_copy(key_in, gathered.at[0, 0, 0], local_sem.at[6]),
        pltpu.make_async_copy(value_in, gathered.at[0, 0, 1], local_sem.at[7]),
        pltpu.make_async_copy(slot_in, slot_ref, local_sem.at[8]),
        pltpu.make_async_copy(step_in, step_ref, local_sem.at[9]),
        pltpu.make_async_copy(slope_in, slope_ref, local_sem.at[10]),
    ]
    for copy in locals_:
        copy.start()
    spare = key_rows - cache_rows - rows
    keys[pl.ds(cache_rows + rows, spare), :] = jnp.zeros((spare, width), jnp.bfloat16)
    values[pl.ds(cache_rows + rows, spare), :] = jnp.zeros((spare, width), jnp.bfloat16)

    pl.semaphore_wait(barrier, owners - 1 + head_devices - 1)

    def wrapped(index, size):
        if size & (size - 1):
            return lax.rem(index + size, size)
        return index & (size - 1)

    def device(dz, dp):
        z = wrapped(my_z + dz, PLANES)
        return (z * plane + wrapped(my_p + dp, plane), my_head)

    def send(source, target, sems, index, where):
        return pltpu.make_async_remote_copy(
            src_ref=source,
            dst_ref=target,
            send_sem=sems[0].at[index],
            recv_sem=sems[1].at[index],
            device_id=where,
            device_id_type=MESH,
        )

    def query_copy(dz, dp):
        slot = dp * PLANES + dz
        sems = (query_send, query_recv)
        return send(query_in, queries.at[slot], sems, slot, device(dz, dp))

    def relay_copy(dp):
        slot = dp * PLANES + 1
        return send(
            queries.at[pl.ds(1, PLANES - 1)],
            queries.at[pl.ds(slot, PLANES - 1)],
            (query_send, query_recv),
            slot,
            device(0, dp),
        )

    def part_copy(dz, dp):
        slot = dp * PLANES + dz
        sems = (part_send, part_recv)
        return send(sent.at[slot], received.at[slot], sems, slot, device(-dz, -dp))

    def col_copy(dz):
        sems = (col_send, col_recv)
        return send(gathered.at[0, 0], gathered.at[0, dz], sems, dz, device(dz, 0))

    def plane_copy(dp):
        sems = (plane_send, plane_recv)
        return send(gathered.at[0], gathered.at[dp], sems, dp, device(0, dp))

    others = [(dz, dp) for dp in range(plane) for dz in range(PLANES) if dz or dp]

    for dz in range(1, PLANES):
        query_copy(dz, 0).start()
    for dp in range(1, plane):
        query_copy(0, dp).start()
    for copy in locals_:
        copy.wait()
    for dz in range(1, PLANES):
        col_copy(dz).start()

    slot_rank = jnp.int32(0)
    for slot in range(owners):
        slot_rank += jnp.where(slot_ref[slot] == me, slot, 0)
    age = (slot_rank + 1).astype(jnp.float32) * (1.0 / owners)
    scale = 1.0 / math.sqrt(head_dim)
    tokens = PLANES * rows
    column = lax.broadcasted_iota(jnp.int32, (1, key_rows), 1)
    lane = lax.broadcasted_iota(jnp.int32, (tokens, LANES), 1)
    group, piece = lane >> 3, lane & 7
    for head in range(heads):
        cut = slice(head * head_dim, (head + 1) * head_dim)
        flat_keys[cut, :] = keys[:, cut].T
        wide_values[head, :, :head_dim] = values[:, cut]
        wide_values[head, :, head_dim:] = jnp.ones((key_rows, LANES), jnp.bfloat16)

    def weigh(dp):
        slots = slice(dp * PLANES, (dp + 1) * PLANES)
        query = queries[slots].reshape(tokens, width)
        stat = jnp.zeros((tokens, LANES), jnp.float32)
        for head in range(heads):
            cut = slice(head * head_dim, (head + 1) * head_dim)
            penalty = jnp.where(
                column < cache_rows,
                slope_ref[head] * age,
                jnp.where(column < cache_rows + rows, 0.0, 1e30),
            )
            scores = (
                jnp.dot(query[:, cut], flat_keys[cut, :], preferred_element_type=jnp.float32)
                * scale
                - penalty
            )
            largest = jnp.max(scores, axis=1, keepdims=True)
            weights = jnp.exp(scores - largest).astype(jnp.bfloat16)
            both = jnp.dot(weights, wide_values[head], preferred_element_type=jnp.float32)
            numer, denom = both[:, :head_dim], both[:, head_dim:]
            sent[slots, :, cut] = numer.astype(jnp.bfloat16).reshape(PLANES, rows, head_dim)
            stat = jnp.where(group == head, jnp.where(piece < 3, largest, denom), stat)
        high = stat.astype(jnp.bfloat16).astype(jnp.float32)
        rest = stat - high
        middle = rest.astype(jnp.bfloat16).astype(jnp.float32)
        low = rest - middle
        third = jnp.where(piece < 3, piece, piece - 3)
        cuts = jnp.where(third == 0, high, jnp.where(third == 1, middle, low))
        sent[slots, :, width:] = cuts.astype(jnp.bfloat16).reshape(PLANES, rows, LANES)

    for dz in range(1, PLANES):
        query_copy(dz, 0).wait_recv()
    for dp in range(1, plane):
        relay_copy(dp).start()

    for dp in range(plane):
        if dp:
            query_copy(0, dp).wait_recv()
            relay_copy(dp).wait_recv()
        weigh(dp)
        for dz in range(0 if dp else 1, PLANES):
            part_copy(dz, dp).start()
    received[0] = sent[0]

    for dz in range(1, PLANES):
        col_copy(dz).wait_recv()
    for dp in range(1, plane):
        plane_copy(dp).start()

    for dz, dp in others:
        part_copy(dz, dp).wait_recv()

    stats = received[:, :, width:].astype(jnp.float32).reshape(owners * rows, LANES)
    stats = (
        stats
        + pltpu.roll(stats, LANES - 1, axis=1)
        + pltpu.roll(stats, LANES - 2, axis=1)
    )
    denoms = pltpu.roll(stats, LANES - 3, axis=1).reshape(owners, rows, LANES)
    maxima = stats.reshape(owners, rows, LANES)
    factor = jnp.exp(maxima - jnp.max(maxima, axis=0, keepdims=True))
    share = factor / jnp.sum(factor * denoms, axis=0, keepdims=True)
    attended = []
    for head in range(heads):
        cut = slice(head * head_dim, (head + 1) * head_dim)
        attended.append(
            jnp.sum(
                share[:, :, 8 * head : 8 * head + 1] * received[:, :, cut].astype(jnp.float32),
                axis=0,
            )
        )
    total = attended[0] * attended[0]
    for block in attended[1:]:
        total += block * block
    squares[0] = jnp.broadcast_to(jnp.sum(total, axis=1, keepdims=True), (rows, LANES))

    def square_copy(step):
        where = (me, wrapped(my_head + step, head_devices))
        return send(squares.at[0], squares.at[step], (square_send, square_recv), step, where)

    for step in range(1, head_devices):
        square_copy(step).start()
    for dz in range(1, PLANES):
        query_copy(dz, 0).wait_send()
        col_copy(dz).wait_send()
    for dp in range(1, plane):
        query_copy(0, dp).wait_send()
        relay_copy(dp).wait_send()
    for dz, dp in others:
        part_copy(dz, dp).wait_send()
    moment = lax.broadcasted_iota(jnp.int32, gate.shape, 0) == step_ref[0]
    gate_row = jnp.sum(jnp.where(moment, gate[...], 0.0), axis=0, keepdims=True)
    for dp in range(1, plane):
        plane_copy(dp).wait_recv()
    for dz in range(PLANES):
        z = wrapped(my_z - dz, PLANES)
        for dp in range(plane):
            p = wrapped(my_p - dp, plane)
            all_keys[z, p] = gathered[dp, dz, 0]
            all_values[z, p] = gathered[dp, dz, 1]
    handed = [
        pltpu.make_async_copy(all_keys, keys_out, local_sem.at[0]),
        pltpu.make_async_copy(all_values, values_out, local_sem.at[1]),
    ]
    for copy in handed:
        copy.start()
    for step in range(1, head_devices):
        square_copy(step).wait_recv()
    mean = jnp.sum(squares[...], axis=0) * (1.0 / (width * head_devices))
    inverse = lax.rsqrt(mean + 1e-06)
    for head in range(heads):
        cut = slice(head * head_dim, (head + 1) * head_dim)
        out_ref[:, cut] = (attended[head] * inverse * gate_row[:, cut]).astype(jnp.bfloat16)

    for step in range(1, head_devices):
        square_copy(step).wait_send()
    for dp in range(1, plane):
        plane_copy(dp).wait_send()
    for copy in handed:
        copy.wait()


def finish(
    evictor_ref,
    attended_in,
    all_keys,
    all_values,
    cache_key_in,
    cache_value_in,
    out_ref,
    next_key,
    next_value,
    attended,
    held,
    sem,
):
    first = pltpu.make_async_copy(attended_in, attended, sem.at[0])
    first.start()

    def roll(key_from, value_from):
        loads = [
            pltpu.make_async_copy(key_from, held.at[0], sem.at[1]),
            pltpu.make_async_copy(value_from, held.at[1], sem.at[2]),
        ]
        stores = [
            pltpu.make_async_copy(held.at[0], next_key, sem.at[1]),
            pltpu.make_async_copy(held.at[1], next_value, sem.at[2]),
        ]
        output = pltpu.make_async_copy(attended, out_ref, sem.at[0])
        for load in loads:
            load.start()
        first.wait()
        output.start()
        for load, store in zip(loads, stores):
            load.wait()
            store.start()
        output.wait()
        for store in stores:
            store.wait()

    evicted = lax.axis_index("ctx") == evictor_ref[0]
    pl.when(evicted)(lambda: roll(all_keys, all_values))
    pl.when(jnp.logical_not(evicted))(lambda: roll(cache_key_in, cache_value_in))


def body(
    fresh_query,
    fresh_key,
    fresh_value,
    cache_key,
    cache_value,
    slot_owner,
    evictor,
    timestep,
    age_slope,
    time_gate,
):
    rows, width = fresh_query.shape
    cache_rows = cache_key.shape[0]
    owners = lax.axis_size("ctx")
    head_devices = lax.axis_size("head")
    plane = owners // PLANES
    heads = age_slope.shape[0]
    key_rows = cache_rows + LANES * pl.cdiv(rows, LANES)
    smem = pl.BlockSpec(memory_space=pltpu.SMEM)
    vmem = pl.BlockSpec(memory_space=pltpu.VMEM)
    anywhere = pl.BlockSpec(memory_space=pltpu.HBM)
    bf16 = jnp.bfloat16
    dma = pltpu.SemaphoreType.DMA
    gathered = jax.ShapeDtypeStruct((PLANES, plane, rows, width), bf16)
    attn_output, fresh_keys, fresh_values = pl.pallas_call(
        functools.partial(kernel, owners, head_devices),
        out_shape=(jax.ShapeDtypeStruct((rows, width), bf16), gathered, gathered),
        in_specs=[anywhere] * 9,
        out_specs=(vmem, anywhere, anywhere),
        scratch_shapes=[
            pltpu.VMEM(gathered.shape, bf16),
            pltpu.VMEM(gathered.shape, bf16),
            pltpu.VMEM((plane, PLANES, 2, rows, width), bf16),
            pltpu.VMEM((owners, rows, width), bf16),
            pltpu.VMEM((key_rows, width), bf16),
            pltpu.VMEM((key_rows, width), bf16),
            pltpu.VMEM(time_gate.shape, jnp.float32),
            pltpu.VMEM((owners, rows, width + LANES), bf16),
            pltpu.VMEM((owners, rows, width + LANES), bf16),
            pltpu.VMEM((head_devices, rows, LANES), jnp.float32),
            pltpu.SMEM(slot_owner.shape, jnp.int32),
            pltpu.SMEM(timestep.shape, jnp.int32),
            pltpu.SMEM(age_slope.shape, jnp.float32),
            pltpu.VMEM((width, key_rows), bf16),
            pltpu.VMEM((heads, key_rows, width // heads + LANES), bf16),
            dma((11,)),
            dma((owners,)),
            dma((owners,)),
            dma((owners,)),
            dma((owners,)),
            dma((PLANES,)),
            dma((PLANES,)),
            dma((plane,)),
            dma((plane,)),
            dma((head_devices,)),
            dma((head_devices,)),
        ],
        compiler_params=pltpu.CompilerParams(
            collective_id=0, has_side_effects=True, vmem_limit_bytes=60 * 1024 * 1024
        ),
        name="attend",
    )(
        slot_owner,
        timestep,
        age_slope,
        fresh_query,
        fresh_key,
        fresh_value,
        cache_key,
        cache_value,
        time_gate,
    )
    cache_shape = jax.ShapeDtypeStruct(cache_key.shape, bf16)
    return pl.pallas_call(
        finish,
        out_shape=(jax.ShapeDtypeStruct((rows, width), bf16), cache_shape, cache_shape),
        in_specs=[smem] + [anywhere] * 5,
        out_specs=(anywhere, anywhere, anywhere),
        scratch_shapes=[
            pltpu.VMEM((rows, width), bf16),
            pltpu.VMEM((2,) + cache_key.shape, bf16),
            dma((3,)),
        ],
        compiler_params=pltpu.CompilerParams(vmem_limit_bytes=60 * 1024 * 1024),
        name="finish",
    )(
        evictor,
        attn_output,
        fresh_keys.reshape(cache_key.shape),
        fresh_values.reshape(cache_value.shape),
        cache_key,
        cache_value,
    )


def solution(mesh):
    return jax.shard_map(
        body,
        mesh=mesh,
        in_specs=(
            P("ctx", "head"),
            P("ctx", "head"),
            P("ctx", "head"),
            P("ctx", "head"),
            P("ctx", "head"),
            P(),
            P(),
            P(),
            P("head"),
            P(None, "head"),
        ),
        out_specs=(P("ctx", "head"), P("ctx", "head"), P("ctx", "head")),
        check_vma=False,
    )
```

```python
import functools
import math

import jax
import jax.numpy as jnp
from jax import lax
from jax.experimental import pallas as pl
from jax.experimental.pallas import tpu as pltpu
from jax.sharding import PartitionSpec as P

MESH = pl.DeviceIdType.MESH
PLANES = 4
LANES = 128


def kernel(
    owners,
    head_devices,
    slot_in,
    step_in,
    slope_in,
    query_in,
    key_in,
    value_in,
    cache_key_in,
    cache_value_in,
    gate_in,
    out_ref,
    keys_out,
    values_out,
    all_keys,
    all_values,
    gathered,
    queries,
    keys,
    values,
    gate,
    sent,
    received,
    squares,
    slot_ref,
    step_ref,
    slope_ref,
    flat_keys,
    wide_values,
    local_sem,
    query_send,
    query_recv,
    part_send,
    part_recv,
    col_send,
    col_recv,
    plane_send,
    plane_recv,
    square_send,
    square_recv,
):
    rows, width = query_in.shape
    cache_rows = cache_key_in.shape[0]
    heads = slope_ref.shape[0]
    head_dim = width // heads
    plane = owners // PLANES
    me = lax.axis_index("ctx")
    my_head = lax.axis_index("head")
    my_z = me // plane
    my_p = lax.rem(me, plane)
    key_rows = keys.shape[0]

    barrier = pltpu.get_barrier_semaphore()

    def greet(step, carry):
        peer = lax.rem(me + step, owners)
        pl.semaphore_signal(barrier, inc=1, device_id=(peer, my_head), device_id_type=MESH)
        return carry

    lax.fori_loop(1, owners, greet, 0)
    for step in range(1, head_devices):
        peer = lax.rem(my_head + step, head_devices)
        pl.semaphore_signal(barrier, inc=1, device_id=(me, peer), device_id_type=MESH)

    locals_ = [
        pltpu.make_async_copy(query_in, queries.at[0], local_sem.at[0]),
        pltpu.make_async_copy(cache_key_in, keys.at[pl.ds(0, cache_rows)], local_sem.at[1]),
        pltpu.make_async_copy(key_in, keys.at[pl.ds(cache_rows, rows)], local_sem.at[2]),
        pltpu.make_async_copy(cache_value_in, values.at[pl.ds(0, cache_rows)], local_sem.at[3]),
        pltpu.make_async_copy(value_in, values.at[pl.ds(cache_rows, rows)], local_sem.at[4]),
        pltpu.make_async_copy(gate_in, gate, local_sem.at[5]),
        pltpu.make_async_copy(key_in, gathered.at[0, 0, 0], local_sem.at[6]),
        pltpu.make_async_copy(value_in, gathered.at[0, 0, 1], local_sem.at[7]),
        pltpu.make_async_copy(slot_in, slot_ref, local_sem.at[8]),
        pltpu.make_async_copy(step_in, step_ref, local_sem.at[9]),
        pltpu.make_async_copy(slope_in, slope_ref, local_sem.at[10]),
    ]
    for copy in locals_:
        copy.start()
    spare = key_rows - cache_rows - rows
    keys[pl.ds(cache_rows + rows, spare), :] = jnp.zeros((spare, width), jnp.bfloat16)
    values[pl.ds(cache_rows + rows, spare), :] = jnp.zeros((spare, width), jnp.bfloat16)

    pl.semaphore_wait(barrier, owners - 1 + head_devices - 1)

    def wrapped(index, size):
        if size & (size - 1):
            return lax.rem(index + size, size)
        return index & (size - 1)

    def device(dz, dp):
        z = wrapped(my_z + dz, PLANES)
        return (z * plane + wrapped(my_p + dp, plane), my_head)

    def send(source, target, sems, index, where):
        return pltpu.make_async_remote_copy(
            src_ref=source,
            dst_ref=target,
            send_sem=sems[0].at[index],
            recv_sem=sems[1].at[index],
            device_id=where,
            device_id_type=MESH,
        )

    def query_copy(dz, dp):
        slot = dp * PLANES + dz
        sems = (query_send, query_recv)
        return send(query_in, queries.at[slot], sems, slot, device(dz, dp))

    def relay_copy(dp):
        slot = dp * PLANES + 1
        return send(
            queries.at[pl.ds(1, PLANES - 1)],
            queries.at[pl.ds(slot, PLANES - 1)],
            (query_send, query_recv),
            slot,
            device(0, dp),
        )

    def part_copy(dz, dp):
        slot = dp * PLANES + dz
        sems = (part_send, part_recv)
        return send(sent.at[slot], received.at[slot], sems, slot, device(-dz, -dp))

    def col_copy(dz):
        sems = (col_send, col_recv)
        return send(gathered.at[0, 0], gathered.at[0, dz], sems, dz, device(dz, 0))

    def plane_copy(dp):
        sems = (plane_send, plane_recv)
        return send(gathered.at[0], gathered.at[dp], sems, dp, device(0, dp))

    others = [(dz, dp) for dp in range(plane) for dz in range(PLANES) if dz or dp]

    for dz in range(1, PLANES):
        query_copy(dz, 0).start()
    for dp in range(1, plane):
        query_copy(0, dp).start()
    for copy in locals_:
        copy.wait()
    for dz in range(1, PLANES):
        col_copy(dz).start()

    slot_rank = jnp.int32(0)
    for slot in range(owners):
        slot_rank += jnp.where(slot_ref[slot] == me, slot, 0)
    age = (slot_rank + 1).astype(jnp.float32) * (1.0 / owners)
    scale = 1.0 / math.sqrt(head_dim)
    tokens = PLANES * rows
    column = lax.broadcasted_iota(jnp.int32, (1, key_rows), 1)
    lane = lax.broadcasted_iota(jnp.int32, (tokens, LANES), 1)
    group, piece = lane >> 3, lane & 7
    for head in range(heads):
        cut = slice(head * head_dim, (head + 1) * head_dim)
        flat_keys[cut, :] = keys[:, cut].T
        wide_values[head, :, :head_dim] = values[:, cut]
        wide_values[head, :, head_dim:] = jnp.ones((key_rows, LANES), jnp.bfloat16)

    def weigh(dp):
        slots = slice(dp * PLANES, (dp + 1) * PLANES)
        query = queries[slots].reshape(tokens, width)
        stat = jnp.zeros((tokens, LANES), jnp.float32)
        for head in range(heads):
            cut = slice(head * head_dim, (head + 1) * head_dim)
            penalty = jnp.where(
                column < cache_rows,
                slope_ref[head] * age,
                jnp.where(column < cache_rows + rows, 0.0, 1e30),
            )
            scores = (
                jnp.dot(query[:, cut], flat_keys[cut, :], preferred_element_type=jnp.float32)
                * scale
                - penalty
            )
            largest = jnp.max(scores, axis=1, keepdims=True)
            weights = jnp.exp(scores - largest).astype(jnp.bfloat16)
            both = jnp.dot(weights, wide_values[head], preferred_element_type=jnp.float32)
            numer, denom = both[:, :head_dim], both[:, head_dim:]
            sent[slots, :, cut] = numer.astype(jnp.bfloat16).reshape(PLANES, rows, head_dim)
            stat = jnp.where(group == head, jnp.where(piece < 3, largest, denom), stat)
        high = stat.astype(jnp.bfloat16).astype(jnp.float32)
        rest = stat - high
        middle = rest.astype(jnp.bfloat16).astype(jnp.float32)
        low = rest - middle
        third = jnp.where(piece < 3, piece, piece - 3)
        cuts = jnp.where(third == 0, high, jnp.where(third == 1, middle, low))
        sent[slots, :, width:] = cuts.astype(jnp.bfloat16).reshape(PLANES, rows, LANES)

    for dz in range(1, PLANES):
        query_copy(dz, 0).wait_recv()
    for dp in range(1, plane):
        relay_copy(dp).start()

    for dp in range(plane):
        if dp:
            query_copy(0, dp).wait_recv()
            relay_copy(dp).wait_recv()
        weigh(dp)
        for dz in range(0 if dp else 1, PLANES):
            part_copy(dz, dp).start()
        if dp == 0:
            for dz in range(1, PLANES):
                col_copy(dz).wait_recv()
            for peer in range(1, plane):
                plane_copy(peer).start()
    received[0] = sent[0]

    for dz, dp in others:
        part_copy(dz, dp).wait_recv()

    stats = received[:, :, width:].astype(jnp.float32).reshape(owners * rows, LANES)
    stats = (
        stats
        + pltpu.roll(stats, LANES - 1, axis=1)
        + pltpu.roll(stats, LANES - 2, axis=1)
    )
    denoms = pltpu.roll(stats, LANES - 3, axis=1).reshape(owners, rows, LANES)
    maxima = stats.reshape(owners, rows, LANES)
    factor = jnp.exp(maxima - jnp.max(maxima, axis=0, keepdims=True))
    share = factor / jnp.sum(factor * denoms, axis=0, keepdims=True)
    attended = []
    for head in range(heads):
        cut = slice(head * head_dim, (head + 1) * head_dim)
        attended.append(
            jnp.sum(
                share[:, :, 8 * head : 8 * head + 1] * received[:, :, cut].astype(jnp.float32),
                axis=0,
            )
        )
    total = attended[0] * attended[0]
    for block in attended[1:]:
        total += block * block
    squares[0] = jnp.broadcast_to(jnp.sum(total, axis=1, keepdims=True), (rows, LANES))

    def square_copy(step):
        where = (me, wrapped(my_head + step, head_devices))
        return send(squares.at[0], squares.at[step], (square_send, square_recv), step, where)

    for step in range(1, head_devices):
        square_copy(step).start()
    for dz in range(1, PLANES):
        query_copy(dz, 0).wait_send()
        col_copy(dz).wait_send()
    for dp in range(1, plane):
        query_copy(0, dp).wait_send()
        relay_copy(dp).wait_send()
    for dz, dp in others:
        part_copy(dz, dp).wait_send()
    moment = lax.broadcasted_iota(jnp.int32, gate.shape, 0) == step_ref[0]
    gate_row = jnp.sum(jnp.where(moment, gate[...], 0.0), axis=0, keepdims=True)
    for dp in range(1, plane):
        plane_copy(dp).wait_recv()
    for dz in range(PLANES):
        z = wrapped(my_z - dz, PLANES)
        for dp in range(plane):
            p = wrapped(my_p - dp, plane)
            all_keys[z, p] = gathered[dp, dz, 0]
            all_values[z, p] = gathered[dp, dz, 1]
    handed = [
        pltpu.make_async_copy(all_keys, keys_out, local_sem.at[0]),
        pltpu.make_async_copy(all_values, values_out, local_sem.at[1]),
    ]
    for copy in handed:
        copy.start()
    for step in range(1, head_devices):
        square_copy(step).wait_recv()
    mean = jnp.sum(squares[...], axis=0) * (1.0 / (width * head_devices))
    inverse = lax.rsqrt(mean + 1e-06)
    for head in range(heads):
        cut = slice(head * head_dim, (head + 1) * head_dim)
        out_ref[:, cut] = (attended[head] * inverse * gate_row[:, cut]).astype(jnp.bfloat16)

    for step in range(1, head_devices):
        square_copy(step).wait_send()
    for dp in range(1, plane):
        plane_copy(dp).wait_send()
    for copy in handed:
        copy.wait()


def finish(
    evictor_ref,
    attended_in,
    all_keys,
    all_values,
    cache_key_in,
    cache_value_in,
    out_ref,
    next_key,
    next_value,
    attended,
    held,
    sem,
):
    first = pltpu.make_async_copy(attended_in, attended, sem.at[0])
    first.start()

    def roll(key_from, value_from):
        loads = [
            pltpu.make_async_copy(key_from, held.at[0], sem.at[1]),
            pltpu.make_async_copy(value_from, held.at[1], sem.at[2]),
        ]
        stores = [
            pltpu.make_async_copy(held.at[0], next_key, sem.at[1]),
            pltpu.make_async_copy(held.at[1], next_value, sem.at[2]),
        ]
        output = pltpu.make_async_copy(attended, out_ref, sem.at[0])
        for load in loads:
            load.start()
        first.wait()
        output.start()
        for load, store in zip(loads, stores):
            load.wait()
            store.start()
        output.wait()
        for store in stores:
            store.wait()

    evicted = lax.axis_index("ctx") == evictor_ref[0]
    pl.when(evicted)(lambda: roll(all_keys, all_values))
    pl.when(jnp.logical_not(evicted))(lambda: roll(cache_key_in, cache_value_in))


def body(
    fresh_query,
    fresh_key,
    fresh_value,
    cache_key,
    cache_value,
    slot_owner,
    evictor,
    timestep,
    age_slope,
    time_gate,
):
    rows, width = fresh_query.shape
    cache_rows = cache_key.shape[0]
    owners = lax.axis_size("ctx")
    head_devices = lax.axis_size("head")
    plane = owners // PLANES
    heads = age_slope.shape[0]
    key_rows = cache_rows + LANES * pl.cdiv(rows, LANES)
    smem = pl.BlockSpec(memory_space=pltpu.SMEM)
    vmem = pl.BlockSpec(memory_space=pltpu.VMEM)
    anywhere = pl.BlockSpec(memory_space=pltpu.HBM)
    bf16 = jnp.bfloat16
    dma = pltpu.SemaphoreType.DMA
    gathered = jax.ShapeDtypeStruct((PLANES, plane, rows, width), bf16)
    attn_output, fresh_keys, fresh_values = pl.pallas_call(
        functools.partial(kernel, owners, head_devices),
        out_shape=(jax.ShapeDtypeStruct((rows, width), bf16), gathered, gathered),
        in_specs=[anywhere] * 9,
        out_specs=(vmem, anywhere, anywhere),
        scratch_shapes=[
            pltpu.VMEM(gathered.shape, bf16),
            pltpu.VMEM(gathered.shape, bf16),
            pltpu.VMEM((plane, PLANES, 2, rows, width), bf16),
            pltpu.VMEM((owners, rows, width), bf16),
            pltpu.VMEM((key_rows, width), bf16),
            pltpu.VMEM((key_rows, width), bf16),
            pltpu.VMEM(time_gate.shape, jnp.float32),
            pltpu.VMEM((owners, rows, width + LANES), bf16),
            pltpu.VMEM((owners, rows, width + LANES), bf16),
            pltpu.VMEM((head_devices, rows, LANES), jnp.float32),
            pltpu.SMEM(slot_owner.shape, jnp.int32),
            pltpu.SMEM(timestep.shape, jnp.int32),
            pltpu.SMEM(age_slope.shape, jnp.float32),
            pltpu.VMEM((width, key_rows), bf16),
            pltpu.VMEM((heads, key_rows, width // heads + LANES), bf16),
            dma((11,)),
            dma((owners,)),
            dma((owners,)),
            dma((owners,)),
            dma((owners,)),
            dma((PLANES,)),
            dma((PLANES,)),
            dma((plane,)),
            dma((plane,)),
            dma((head_devices,)),
            dma((head_devices,)),
        ],
        compiler_params=pltpu.CompilerParams(
            collective_id=0, has_side_effects=True, vmem_limit_bytes=60 * 1024 * 1024
        ),
        name="attend",
    )(
        slot_owner,
        timestep,
        age_slope,
        fresh_query,
        fresh_key,
        fresh_value,
        cache_key,
        cache_value,
        time_gate,
    )
    cache_shape = jax.ShapeDtypeStruct(cache_key.shape, bf16)
    return pl.pallas_call(
        finish,
        out_shape=(jax.ShapeDtypeStruct((rows, width), bf16), cache_shape, cache_shape),
        in_specs=[smem] + [anywhere] * 5,
        out_specs=(anywhere, anywhere, anywhere),
        scratch_shapes=[
            pltpu.VMEM((rows, width), bf16),
            pltpu.VMEM((2,) + cache_key.shape, bf16),
            dma((3,)),
        ],
        compiler_params=pltpu.CompilerParams(vmem_limit_bytes=60 * 1024 * 1024),
        name="finish",
    )(
        evictor,
        attn_output,
        fresh_keys.reshape(cache_key.shape),
        fresh_values.reshape(cache_value.shape),
        cache_key,
        cache_value,
    )


def solution(mesh):
    return jax.shard_map(
        body,
        mesh=mesh,
        in_specs=(
            P("ctx", "head"),
            P("ctx", "head"),
            P("ctx", "head"),
            P("ctx", "head"),
            P("ctx", "head"),
            P(),
            P(),
            P(),
            P("head"),
            P(None, "head"),
        ),
        out_specs=(P("ctx", "head"), P("ctx", "head"), P("ctx", "head")),
        check_vma=False,
    )
```

```python
import functools
import math

import jax
import jax.numpy as jnp
from jax import lax
from jax.experimental import pallas as pl
from jax.experimental.pallas import tpu as pltpu
from jax.sharding import PartitionSpec as P

MESH = pl.DeviceIdType.MESH
PLANES = 4
LANES = 128


def kernel(
    owners,
    head_devices,
    slot_in,
    step_in,
    slope_in,
    query_in,
    key_in,
    value_in,
    cache_key_in,
    cache_value_in,
    gate_in,
    out_ref,
    keys_out,
    values_out,
    all_keys,
    all_values,
    gathered,
    queries,
    keys,
    values,
    gate,
    sent,
    received,
    squares,
    slot_ref,
    step_ref,
    slope_ref,
    flat_keys,
    wide_values,
    local_sem,
    query_send,
    query_recv,
    part_send,
    part_recv,
    col_send,
    col_recv,
    plane_send,
    plane_recv,
    square_send,
    square_recv,
):
    rows, width = query_in.shape
    cache_rows = cache_key_in.shape[0]
    heads = slope_ref.shape[0]
    head_dim = width // heads
    plane = owners // PLANES
    me = lax.axis_index("ctx")
    my_head = lax.axis_index("head")
    my_z = me // plane
    my_p = lax.rem(me, plane)
    key_rows = keys.shape[0]

    barrier = pltpu.get_barrier_semaphore()

    def greet(step, carry):
        peer = lax.rem(me + step, owners)
        pl.semaphore_signal(barrier, inc=1, device_id=(peer, my_head), device_id_type=MESH)
        return carry

    lax.fori_loop(1, owners, greet, 0)
    for step in range(1, head_devices):
        peer = lax.rem(my_head + step, head_devices)
        pl.semaphore_signal(barrier, inc=1, device_id=(me, peer), device_id_type=MESH)

    locals_ = [
        pltpu.make_async_copy(query_in, queries.at[0], local_sem.at[0]),
        pltpu.make_async_copy(cache_key_in, keys.at[pl.ds(0, cache_rows)], local_sem.at[1]),
        pltpu.make_async_copy(key_in, keys.at[pl.ds(cache_rows, rows)], local_sem.at[2]),
        pltpu.make_async_copy(cache_value_in, values.at[pl.ds(0, cache_rows)], local_sem.at[3]),
        pltpu.make_async_copy(value_in, values.at[pl.ds(cache_rows, rows)], local_sem.at[4]),
        pltpu.make_async_copy(gate_in, gate, local_sem.at[5]),
        pltpu.make_async_copy(key_in, gathered.at[0, 0, 0], local_sem.at[6]),
        pltpu.make_async_copy(value_in, gathered.at[0, 0, 1], local_sem.at[7]),
        pltpu.make_async_copy(slot_in, slot_ref, local_sem.at[8]),
        pltpu.make_async_copy(step_in, step_ref, local_sem.at[9]),
        pltpu.make_async_copy(slope_in, slope_ref, local_sem.at[10]),
    ]
    for copy in locals_:
        copy.start()
    spare = key_rows - cache_rows - rows
    keys[pl.ds(cache_rows + rows, spare), :] = jnp.zeros((spare, width), jnp.bfloat16)
    values[pl.ds(cache_rows + rows, spare), :] = jnp.zeros((spare, width), jnp.bfloat16)

    pl.semaphore_wait(barrier, owners - 1 + head_devices - 1)

    def wrapped(index, size):
        if size & (size - 1):
            return lax.rem(index + size, size)
        return index & (size - 1)

    def device(dz, dp):
        z = wrapped(my_z + dz, PLANES)
        return (z * plane + wrapped(my_p + dp, plane), my_head)

    def send(source, target, sems, index, where):
        return pltpu.make_async_remote_copy(
            src_ref=source,
            dst_ref=target,
            send_sem=sems[0].at[index],
            recv_sem=sems[1].at[index],
            device_id=where,
            device_id_type=MESH,
        )

    def query_copy(dz, dp):
        slot = dp * PLANES + dz
        sems = (query_send, query_recv)
        return send(query_in, queries.at[slot], sems, slot, device(dz, dp))

    def relay_copy(dp):
        slot = dp * PLANES + 1
        return send(
            queries.at[pl.ds(1, PLANES - 1)],
            queries.at[pl.ds(slot, PLANES - 1)],
            (query_send, query_recv),
            slot,
            device(0, dp),
        )

    def part_copy(dz, dp):
        slot = dp * PLANES + dz
        sems = (part_send, part_recv)
        return send(sent.at[slot], received.at[slot], sems, slot, device(-dz, -dp))

    def col_copy(dz):
        sems = (col_send, col_recv)
        return send(gathered.at[0, 0], gathered.at[0, dz], sems, dz, device(dz, 0))

    def plane_copy(dp):
        sems = (plane_send, plane_recv)
        return send(gathered.at[0], gathered.at[dp], sems, dp, device(0, dp))

    others = [(dz, dp) for dp in range(plane) for dz in range(PLANES) if dz or dp]

    for dz in range(1, PLANES):
        query_copy(dz, 0).start()
    for dp in range(1, plane):
        query_copy(0, dp).start()
    for copy in locals_:
        copy.wait()
    for dz in range(1, PLANES):
        col_copy(dz).start()

    slot_rank = jnp.int32(0)
    for slot in range(owners):
        slot_rank += jnp.where(slot_ref[slot] == me, slot, 0)
    age = (slot_rank + 1).astype(jnp.float32) * (1.0 / owners)
    scale = 1.0 / math.sqrt(head_dim)
    column = lax.broadcasted_iota(jnp.int32, (1, key_rows), 1)
    lane = lax.broadcasted_iota(jnp.int32, (1, LANES), 1)
    group, piece = lane >> 3, lane & 7
    for head in range(heads):
        cut = slice(head * head_dim, (head + 1) * head_dim)
        flat_keys[cut, :] = keys[:, cut].T
        wide_values[head, :, :head_dim] = values[:, cut]
        wide_values[head, :, head_dim:] = jnp.ones((key_rows, LANES), jnp.bfloat16)

    def weigh(columns):
        count = len(columns) * PLANES
        tokens = count * rows
        slots = slice(columns[0] * PLANES, columns[0] * PLANES + count)
        query = queries[slots].reshape(tokens, width)
        stat = jnp.zeros((tokens, LANES), jnp.float32)
        for head in range(heads):
            cut = slice(head * head_dim, (head + 1) * head_dim)
            penalty = jnp.where(
                column < cache_rows,
                slope_ref[head] * age,
                jnp.where(column < cache_rows + rows, 0.0, 1e30),
            )
            scores = (
                jnp.dot(query[:, cut], flat_keys[cut, :], preferred_element_type=jnp.float32)
                * scale
                - penalty
            )
            largest = jnp.max(scores, axis=1, keepdims=True)
            weights = jnp.exp(scores - largest).astype(jnp.bfloat16)
            both = jnp.dot(weights, wide_values[head], preferred_element_type=jnp.float32)
            numer, denom = both[:, :head_dim], both[:, head_dim:]
            sent[slots, :, cut] = numer.astype(jnp.bfloat16).reshape(count, rows, head_dim)
            stat = jnp.where(group == head, jnp.where(piece < 3, largest, denom), stat)
        high = stat.astype(jnp.bfloat16).astype(jnp.float32)
        rest = stat - high
        middle = rest.astype(jnp.bfloat16).astype(jnp.float32)
        low = rest - middle
        third = jnp.where(piece < 3, piece, piece - 3)
        cuts = jnp.where(third == 0, high, jnp.where(third == 1, middle, low))
        sent[slots, :, width:] = cuts.astype(jnp.bfloat16).reshape(count, rows, LANES)

    for dz in range(1, PLANES):
        query_copy(dz, 0).wait_recv()
    for dp in range(1, plane):
        relay_copy(dp).start()

    batches = [range(1)] + [range(dp, min(dp + 3, plane)) for dp in range(1, plane, 3)]
    for columns in batches:
        for dp in columns:
            if dp:
                query_copy(0, dp).wait_recv()
                relay_copy(dp).wait_recv()
        weigh(columns)
        for dp in columns:
            for dz in range(0 if dp else 1, PLANES):
                part_copy(dz, dp).start()
    received[0] = sent[0]

    for dz in range(1, PLANES):
        col_copy(dz).wait_recv()
    for dp in range(1, plane):
        plane_copy(dp).start()

    for dz, dp in others:
        part_copy(dz, dp).wait_recv()

    stats = received[:, :, width:].astype(jnp.float32).reshape(owners * rows, LANES)
    stats = (
        stats
        + pltpu.roll(stats, LANES - 1, axis=1)
        + pltpu.roll(stats, LANES - 2, axis=1)
    )
    denoms = pltpu.roll(stats, LANES - 3, axis=1).reshape(owners, rows, LANES)
    maxima = stats.reshape(owners, rows, LANES)
    factor = jnp.exp(maxima - jnp.max(maxima, axis=0, keepdims=True))
    share = factor / jnp.sum(factor * denoms, axis=0, keepdims=True)
    attended = []
    for head in range(heads):
        cut = slice(head * head_dim, (head + 1) * head_dim)
        attended.append(
            jnp.sum(
                share[:, :, 8 * head : 8 * head + 1] * received[:, :, cut].astype(jnp.float32),
                axis=0,
            )
        )
    total = attended[0] * attended[0]
    for block in attended[1:]:
        total += block * block
    squares[0] = jnp.broadcast_to(jnp.sum(total, axis=1, keepdims=True), (rows, LANES))

    def square_copy(step):
        where = (me, wrapped(my_head + step, head_devices))
        return send(squares.at[0], squares.at[step], (square_send, square_recv), step, where)

    for step in range(1, head_devices):
        square_copy(step).start()
    for dz in range(1, PLANES):
        query_copy(dz, 0).wait_send()
        col_copy(dz).wait_send()
    for dp in range(1, plane):
        query_copy(0, dp).wait_send()
        relay_copy(dp).wait_send()
    for dz, dp in others:
        part_copy(dz, dp).wait_send()
    moment = lax.broadcasted_iota(jnp.int32, gate.shape, 0) == step_ref[0]
    gate_row = jnp.sum(jnp.where(moment, gate[...], 0.0), axis=0, keepdims=True)
    for dp in range(1, plane):
        plane_copy(dp).wait_recv()
    for dz in range(PLANES):
        z = wrapped(my_z - dz, PLANES)
        for dp in range(plane):
            p = wrapped(my_p - dp, plane)
            all_keys[z, p] = gathered[dp, dz, 0]
            all_values[z, p] = gathered[dp, dz, 1]
    handed = [
        pltpu.make_async_copy(all_keys, keys_out, local_sem.at[0]),
        pltpu.make_async_copy(all_values, values_out, local_sem.at[1]),
    ]
    for copy in handed:
        copy.start()
    for step in range(1, head_devices):
        square_copy(step).wait_recv()
    mean = jnp.sum(squares[...], axis=0) * (1.0 / (width * head_devices))
    inverse = lax.rsqrt(mean + 1e-06)
    for head in range(heads):
        cut = slice(head * head_dim, (head + 1) * head_dim)
        out_ref[:, cut] = (attended[head] * inverse * gate_row[:, cut]).astype(jnp.bfloat16)

    for step in range(1, head_devices):
        square_copy(step).wait_send()
    for dp in range(1, plane):
        plane_copy(dp).wait_send()
    for copy in handed:
        copy.wait()


def finish(
    evictor_ref,
    attended_in,
    all_keys,
    all_values,
    cache_key_in,
    cache_value_in,
    out_ref,
    next_key,
    next_value,
    attended,
    held,
    sem,
):
    first = pltpu.make_async_copy(attended_in, attended, sem.at[0])
    first.start()

    def roll(key_from, value_from):
        loads = [
            pltpu.make_async_copy(key_from, held.at[0], sem.at[1]),
            pltpu.make_async_copy(value_from, held.at[1], sem.at[2]),
        ]
        stores = [
            pltpu.make_async_copy(held.at[0], next_key, sem.at[1]),
            pltpu.make_async_copy(held.at[1], next_value, sem.at[2]),
        ]
        output = pltpu.make_async_copy(attended, out_ref, sem.at[0])
        for load in loads:
            load.start()
        first.wait()
        output.start()
        for load, store in zip(loads, stores):
            load.wait()
            store.start()
        output.wait()
        for store in stores:
            store.wait()

    evicted = lax.axis_index("ctx") == evictor_ref[0]
    pl.when(evicted)(lambda: roll(all_keys, all_values))
    pl.when(jnp.logical_not(evicted))(lambda: roll(cache_key_in, cache_value_in))


def body(
    fresh_query,
    fresh_key,
    fresh_value,
    cache_key,
    cache_value,
    slot_owner,
    evictor,
    timestep,
    age_slope,
    time_gate,
):
    rows, width = fresh_query.shape
    cache_rows = cache_key.shape[0]
    owners = lax.axis_size("ctx")
    head_devices = lax.axis_size("head")
    plane = owners // PLANES
    heads = age_slope.shape[0]
    key_rows = cache_rows + LANES * pl.cdiv(rows, LANES)
    smem = pl.BlockSpec(memory_space=pltpu.SMEM)
    vmem = pl.BlockSpec(memory_space=pltpu.VMEM)
    anywhere = pl.BlockSpec(memory_space=pltpu.HBM)
    bf16 = jnp.bfloat16
    dma = pltpu.SemaphoreType.DMA
    gathered = jax.ShapeDtypeStruct((PLANES, plane, rows, width), bf16)
    attn_output, fresh_keys, fresh_values = pl.pallas_call(
        functools.partial(kernel, owners, head_devices),
        out_shape=(jax.ShapeDtypeStruct((rows, width), bf16), gathered, gathered),
        in_specs=[anywhere] * 9,
        out_specs=(vmem, anywhere, anywhere),
        scratch_shapes=[
            pltpu.VMEM(gathered.shape, bf16),
            pltpu.VMEM(gathered.shape, bf16),
            pltpu.VMEM((plane, PLANES, 2, rows, width), bf16),
            pltpu.VMEM((owners, rows, width), bf16),
            pltpu.VMEM((key_rows, width), bf16),
            pltpu.VMEM((key_rows, width), bf16),
            pltpu.VMEM(time_gate.shape, jnp.float32),
            pltpu.VMEM((owners, rows, width + LANES), bf16),
            pltpu.VMEM((owners, rows, width + LANES), bf16),
            pltpu.VMEM((head_devices, rows, LANES), jnp.float32),
            pltpu.SMEM(slot_owner.shape, jnp.int32),
            pltpu.SMEM(timestep.shape, jnp.int32),
            pltpu.SMEM(age_slope.shape, jnp.float32),
            pltpu.VMEM((width, key_rows), bf16),
            pltpu.VMEM((heads, key_rows, width // heads + LANES), bf16),
            dma((11,)),
            dma((owners,)),
            dma((owners,)),
            dma((owners,)),
            dma((owners,)),
            dma((PLANES,)),
            dma((PLANES,)),
            dma((plane,)),
            dma((plane,)),
            dma((head_devices,)),
            dma((head_devices,)),
        ],
        compiler_params=pltpu.CompilerParams(
            collective_id=0, has_side_effects=True, vmem_limit_bytes=60 * 1024 * 1024
        ),
        name="attend",
    )(
        slot_owner,
        timestep,
        age_slope,
        fresh_query,
        fresh_key,
        fresh_value,
        cache_key,
        cache_value,
        time_gate,
    )
    cache_shape = jax.ShapeDtypeStruct(cache_key.shape, bf16)
    return pl.pallas_call(
        finish,
        out_shape=(jax.ShapeDtypeStruct((rows, width), bf16), cache_shape, cache_shape),
        in_specs=[smem] + [anywhere] * 5,
        out_specs=(anywhere, anywhere, anywhere),
        scratch_shapes=[
            pltpu.VMEM((rows, width), bf16),
            pltpu.VMEM((2,) + cache_key.shape, bf16),
            dma((3,)),
        ],
        compiler_params=pltpu.CompilerParams(vmem_limit_bytes=60 * 1024 * 1024),
        name="finish",
    )(
        evictor,
        attn_output,
        fresh_keys.reshape(cache_key.shape),
        fresh_values.reshape(cache_value.shape),
        cache_key,
        cache_value,
    )


def solution(mesh):
    return jax.shard_map(
        body,
        mesh=mesh,
        in_specs=(
            P("ctx", "head"),
            P("ctx", "head"),
            P("ctx", "head"),
            P("ctx", "head"),
            P("ctx", "head"),
            P(),
            P(),
            P(),
            P("head"),
            P(None, "head"),
        ),
        out_specs=(P("ctx", "head"), P("ctx", "head"), P("ctx", "head")),
        check_vma=False,
    )
```

```python
import functools
import math

import jax
import jax.numpy as jnp
from jax import lax
from jax.experimental import pallas as pl
from jax.experimental.pallas import tpu as pltpu
from jax.sharding import PartitionSpec as P

MESH = pl.DeviceIdType.MESH
PLANES = 4
LANES = 128


def kernel(
    owners,
    head_devices,
    slot_in,
    step_in,
    slope_in,
    query_in,
    key_in,
    value_in,
    cache_key_in,
    cache_value_in,
    gate_in,
    out_ref,
    keys_out,
    values_out,
    all_keys,
    all_values,
    gath_key,
    gath_value,
    queries,
    keys,
    values,
    gate,
    sent,
    received,
    squares,
    slot_ref,
    step_ref,
    slope_ref,
    flat_keys,
    wide_values,
    local_sem,
    query_send,
    query_recv,
    part_send,
    part_recv,
    col_send,
    col_recv,
    plane_send,
    plane_recv,
    square_send,
    square_recv,
):
    rows, width = query_in.shape
    cache_rows = cache_key_in.shape[0]
    heads = slope_ref.shape[0]
    head_dim = width // heads
    plane = owners // PLANES
    me = lax.axis_index("ctx")
    my_head = lax.axis_index("head")
    my_z = me // plane
    my_p = lax.rem(me, plane)
    key_rows = keys.shape[0]

    barrier = pltpu.get_barrier_semaphore()

    def greet(step, carry):
        peer = lax.rem(me + step, owners)
        pl.semaphore_signal(barrier, inc=1, device_id=(peer, my_head), device_id_type=MESH)
        return carry

    lax.fori_loop(1, owners, greet, 0)
    for step in range(1, head_devices):
        peer = lax.rem(my_head + step, head_devices)
        pl.semaphore_signal(barrier, inc=1, device_id=(me, peer), device_id_type=MESH)

    locals_ = [
        pltpu.make_async_copy(query_in, queries.at[0], local_sem.at[0]),
        pltpu.make_async_copy(cache_key_in, keys.at[pl.ds(0, cache_rows)], local_sem.at[1]),
        pltpu.make_async_copy(key_in, keys.at[pl.ds(cache_rows, rows)], local_sem.at[2]),
        pltpu.make_async_copy(cache_value_in, values.at[pl.ds(0, cache_rows)], local_sem.at[3]),
        pltpu.make_async_copy(value_in, values.at[pl.ds(cache_rows, rows)], local_sem.at[4]),
        pltpu.make_async_copy(gate_in, gate, local_sem.at[5]),
        pltpu.make_async_copy(key_in, gath_key.at[0, 0], local_sem.at[6]),
        pltpu.make_async_copy(value_in, gath_value.at[0, 0], local_sem.at[7]),
        pltpu.make_async_copy(slot_in, slot_ref, local_sem.at[8]),
        pltpu.make_async_copy(step_in, step_ref, local_sem.at[9]),
        pltpu.make_async_copy(slope_in, slope_ref, local_sem.at[10]),
    ]
    for copy in locals_:
        copy.start()
    spare = key_rows - cache_rows - rows
    keys[pl.ds(cache_rows + rows, spare), :] = jnp.zeros((spare, width), jnp.bfloat16)
    values[pl.ds(cache_rows + rows, spare), :] = jnp.zeros((spare, width), jnp.bfloat16)

    pl.semaphore_wait(barrier, owners - 1 + head_devices - 1)

    def device(dz, dp):
        z = lax.rem(my_z + dz + PLANES, PLANES)
        return (z * plane + lax.rem(my_p + dp + plane, plane), my_head)

    def query_copy(dz, dp, relayed=False):
        slot = dp * PLANES + dz
        return pltpu.make_async_remote_copy(
            src_ref=queries.at[dz] if relayed else query_in,
            dst_ref=queries.at[slot],
            send_sem=query_send.at[slot],
            recv_sem=query_recv.at[slot],
            device_id=device(0 if relayed else dz, dp),
            device_id_type=MESH,
        )

    def part_copy(dz, dp):
        slot = dp * PLANES + dz
        return pltpu.make_async_remote_copy(
            src_ref=sent.at[slot],
            dst_ref=received.at[slot],
            send_sem=part_send.at[slot],
            recv_sem=part_recv.at[slot],
            device_id=device(-dz, -dp),
            device_id_type=MESH,
        )

    def col_copy(kind, dz):
        return pltpu.make_async_remote_copy(
            src_ref=(key_in, value_in)[kind],
            dst_ref=(gath_key, gath_value)[kind].at[0, dz],
            send_sem=col_send.at[kind * PLANES + dz],
            recv_sem=col_recv.at[kind * PLANES + dz],
            device_id=device(dz, 0),
            device_id_type=MESH,
        )

    def plane_copy(kind, dp):
        gathered = (gath_key, gath_value)[kind]
        return pltpu.make_async_remote_copy(
            src_ref=gathered.at[0],
            dst_ref=gathered.at[dp],
            send_sem=plane_send.at[kind * plane + dp],
            recv_sem=plane_recv.at[kind * plane + dp],
            device_id=device(0, dp),
            device_id_type=MESH,
        )

    others = [(dz, dp) for dp in range(plane) for dz in range(PLANES) if dz or dp]

    for dz in range(1, PLANES):
        query_copy(dz, 0).start()
    for dp in range(1, plane):
        query_copy(0, dp).start()

    for copy in locals_:
        copy.wait()
    slot_rank = jnp.int32(0)
    for slot in range(owners):
        slot_rank += jnp.where(slot_ref[slot] == me, slot, 0)
    age = (slot_rank + 1).astype(jnp.float32) * (1.0 / owners)
    scale = 1.0 / math.sqrt(head_dim)
    tokens = PLANES * rows
    column = lax.broadcasted_iota(jnp.int32, (1, key_rows), 1)
    lane = lax.broadcasted_iota(jnp.int32, (tokens, LANES), 1)
    group, piece = lane >> 3, lane & 7
    for head in range(heads):
        cut = slice(head * head_dim, (head + 1) * head_dim)
        flat_keys[cut, :] = keys[:, cut].T
        wide_values[head, :, :head_dim] = values[:, cut]
        wide_values[head, :, head_dim:] = jnp.ones((key_rows, LANES), jnp.bfloat16)

    def weigh(dp):
        slots = slice(dp * PLANES, (dp + 1) * PLANES)
        query = queries[slots].reshape(tokens, width)
        stat = jnp.zeros((tokens, LANES), jnp.float32)
        for head in range(heads):
            cut = slice(head * head_dim, (head + 1) * head_dim)
            penalty = jnp.where(
                column < cache_rows,
                slope_ref[head] * age,
                jnp.where(column < cache_rows + rows, 0.0, 1e30),
            )
            scores = (
                jnp.dot(query[:, cut], flat_keys[cut, :], preferred_element_type=jnp.float32)
                * scale
                - penalty
            )
            largest = jnp.max(scores, axis=1, keepdims=True)
            weights = jnp.exp(scores - largest).astype(jnp.bfloat16)
            both = jnp.dot(weights, wide_values[head], preferred_element_type=jnp.float32)
            numer, denom = both[:, :head_dim], both[:, head_dim:]
            sent[slots, :, cut] = numer.astype(jnp.bfloat16).reshape(PLANES, rows, head_dim)
            stat = jnp.where(group == head, jnp.where(piece < 3, largest, denom), stat)
        high = stat.astype(jnp.bfloat16).astype(jnp.float32)
        rest = stat - high
        middle = rest.astype(jnp.bfloat16).astype(jnp.float32)
        low = rest - middle
        third = jnp.where(piece < 3, piece, piece - 3)
        cuts = jnp.where(third == 0, high, jnp.where(third == 1, middle, low))
        sent[slots, :, width:] = cuts.astype(jnp.bfloat16).reshape(PLANES, rows, LANES)

    for dz in range(1, PLANES):
        query_copy(dz, 0).wait_recv()
        for dp in range(1, plane):
            query_copy(dz, dp, relayed=True).start()
    for dz in range(1, PLANES):
        for kind in range(2):
            col_copy(kind, dz).start()

    for dp in range(plane):
        if dp:
            for dz in range(PLANES):
                query_copy(dz, dp).wait_recv()
        weigh(dp)
        for dz in range(0 if dp else 1, PLANES):
            part_copy(dz, dp).start()
    received[0] = sent[0]

    for kind in range(2):
        for dz in range(1, PLANES):
            col_copy(kind, dz).wait_recv()
        for dp in range(1, plane):
            plane_copy(kind, dp).start()

    for dz, dp in others:
        part_copy(dz, dp).wait_recv()

    stats = received[:, :, width:].astype(jnp.float32).reshape(owners * rows, LANES)
    stats = (
        stats
        + pltpu.roll(stats, LANES - 1, axis=1)
        + pltpu.roll(stats, LANES - 2, axis=1)
    )
    denoms = pltpu.roll(stats, LANES - 3, axis=1).reshape(owners, rows, LANES)
    maxima = stats.reshape(owners, rows, LANES)
    factor = jnp.exp(maxima - jnp.max(maxima, axis=0, keepdims=True))
    share = factor / jnp.sum(factor * denoms, axis=0, keepdims=True)
    attended = []
    for head in range(heads):
        cut = slice(head * head_dim, (head + 1) * head_dim)
        attended.append(
            jnp.sum(
                share[:, :, 8 * head : 8 * head + 1] * received[:, :, cut].astype(jnp.float32),
                axis=0,
            )
        )
    total = attended[0] * attended[0]
    for block in attended[1:]:
        total += block * block
    squares[0] = jnp.broadcast_to(jnp.sum(total, axis=1, keepdims=True), (rows, LANES))

    def square_copy(step):
        return pltpu.make_async_remote_copy(
            src_ref=squares.at[0],
            dst_ref=squares.at[step],
            send_sem=square_send.at[step],
            recv_sem=square_recv.at[step],
            device_id=(me, lax.rem(my_head + step, head_devices)),
            device_id_type=MESH,
        )

    for step in range(1, head_devices):
        square_copy(step).start()
    for dz, dp in others:
        query_copy(dz, dp).wait_send()
        part_copy(dz, dp).wait_send()
    moment = lax.broadcasted_iota(jnp.int32, gate.shape, 0) == step_ref[0]
    gate_row = jnp.sum(jnp.where(moment, gate[...], 0.0), axis=0, keepdims=True)
    for kind in range(2):
        for dz in range(1, PLANES):
            col_copy(kind, dz).wait_send()
        for dp in range(1, plane):
            plane_copy(kind, dp).wait_recv()
    for dz in range(PLANES):
        z = lax.rem(my_z - dz + PLANES, PLANES)
        for dp in range(plane):
            p = lax.rem(my_p - dp + plane, plane)
            all_keys[z, p] = gath_key[dp, dz]
            all_values[z, p] = gath_value[dp, dz]
    handed = [
        pltpu.make_async_copy(all_keys, keys_out, local_sem.at[0]),
        pltpu.make_async_copy(all_values, values_out, local_sem.at[1]),
    ]
    for copy in handed:
        copy.start()
    for step in range(1, head_devices):
        square_copy(step).wait_recv()
    mean = jnp.sum(squares[...], axis=0) * (1.0 / (width * head_devices))
    inverse = lax.rsqrt(mean + 1e-06)
    for head in range(heads):
        cut = slice(head * head_dim, (head + 1) * head_dim)
        out_ref[:, cut] = (attended[head] * inverse * gate_row[:, cut]).astype(jnp.bfloat16)

    for step in range(1, head_devices):
        square_copy(step).wait_send()
    for kind in range(2):
        for dp in range(1, plane):
            plane_copy(kind, dp).wait_send()
    for copy in handed:
        copy.wait()


def finish(
    evictor_ref,
    attended_in,
    all_keys,
    all_values,
    cache_key_in,
    cache_value_in,
    out_ref,
    next_key,
    next_value,
    attended,
    held,
    sem,
):
    first = pltpu.make_async_copy(attended_in, attended, sem.at[0])
    first.start()

    def roll(key_from, value_from):
        loads = [
            pltpu.make_async_copy(key_from, held.at[0], sem.at[1]),
            pltpu.make_async_copy(value_from, held.at[1], sem.at[2]),
        ]
        stores = [
            pltpu.make_async_copy(held.at[0], next_key, sem.at[1]),
            pltpu.make_async_copy(held.at[1], next_value, sem.at[2]),
        ]
        output = pltpu.make_async_copy(attended, out_ref, sem.at[0])
        for load in loads:
            load.start()
        first.wait()
        output.start()
        for load, store in zip(loads, stores):
            load.wait()
            store.start()
        output.wait()
        for store in stores:
            store.wait()

    evicted = lax.axis_index("ctx") == evictor_ref[0]
    pl.when(evicted)(lambda: roll(all_keys, all_values))
    pl.when(jnp.logical_not(evicted))(lambda: roll(cache_key_in, cache_value_in))


def body(
    fresh_query,
    fresh_key,
    fresh_value,
    cache_key,
    cache_value,
    slot_owner,
    evictor,
    timestep,
    age_slope,
    time_gate,
):
    rows, width = fresh_query.shape
    cache_rows = cache_key.shape[0]
    owners = lax.axis_size("ctx")
    head_devices = lax.axis_size("head")
    plane = owners // PLANES
    heads = age_slope.shape[0]
    key_rows = cache_rows + LANES * pl.cdiv(rows, LANES)
    smem = pl.BlockSpec(memory_space=pltpu.SMEM)
    vmem = pl.BlockSpec(memory_space=pltpu.VMEM)
    anywhere = pl.BlockSpec(memory_space=pltpu.HBM)
    bf16 = jnp.bfloat16
    dma = pltpu.SemaphoreType.DMA
    gathered = jax.ShapeDtypeStruct((PLANES, plane, rows, width), bf16)
    attn_output, fresh_keys, fresh_values = pl.pallas_call(
        functools.partial(kernel, owners, head_devices),
        out_shape=(jax.ShapeDtypeStruct((rows, width), bf16), gathered, gathered),
        in_specs=[anywhere] * 9,
        out_specs=(vmem, anywhere, anywhere),
        scratch_shapes=[
            pltpu.VMEM(gathered.shape, bf16),
            pltpu.VMEM(gathered.shape, bf16),
            pltpu.VMEM((plane, PLANES, rows, width), bf16),
            pltpu.VMEM((plane, PLANES, rows, width), bf16),
            pltpu.VMEM((owners, rows, width), bf16),
            pltpu.VMEM((key_rows, width), bf16),
            pltpu.VMEM((key_rows, width), bf16),
            pltpu.VMEM(time_gate.shape, jnp.float32),
            pltpu.VMEM((owners, rows, width + LANES), bf16),
            pltpu.VMEM((owners, rows, width + LANES), bf16),
            pltpu.VMEM((head_devices, rows, LANES), jnp.float32),
            pltpu.SMEM(slot_owner.shape, jnp.int32),
            pltpu.SMEM(timestep.shape, jnp.int32),
            pltpu.SMEM(age_slope.shape, jnp.float32),
            pltpu.VMEM((width, key_rows), bf16),
            pltpu.VMEM((heads, key_rows, width // heads + LANES), bf16),
            dma((11,)),
            dma((owners,)),
            dma((owners,)),
            dma((owners,)),
            dma((owners,)),
            dma((2 * PLANES,)),
            dma((2 * PLANES,)),
            dma((2 * plane,)),
            dma((2 * plane,)),
            dma((head_devices,)),
            dma((head_devices,)),
        ],
        compiler_params=pltpu.CompilerParams(
            collective_id=0, has_side_effects=True, vmem_limit_bytes=60 * 1024 * 1024
        ),
        name="attend",
    )(
        slot_owner,
        timestep,
        age_slope,
        fresh_query,
        fresh_key,
        fresh_value,
        cache_key,
        cache_value,
        time_gate,
    )
    cache_shape = jax.ShapeDtypeStruct(cache_key.shape, bf16)
    return pl.pallas_call(
        finish,
        out_shape=(jax.ShapeDtypeStruct((rows, width), bf16), cache_shape, cache_shape),
        in_specs=[smem] + [anywhere] * 5,
        out_specs=(anywhere, anywhere, anywhere),
        scratch_shapes=[
            pltpu.VMEM((rows, width), bf16),
            pltpu.VMEM((2,) + cache_key.shape, bf16),
            dma((3,)),
        ],
        compiler_params=pltpu.CompilerParams(vmem_limit_bytes=60 * 1024 * 1024),
        name="finish",
    )(
        evictor,
        attn_output,
        fresh_keys.reshape(cache_key.shape),
        fresh_values.reshape(cache_value.shape),
        cache_key,
        cache_value,
    )


def solution(mesh):
    return jax.shard_map(
        body,
        mesh=mesh,
        in_specs=(
            P("ctx", "head"),
            P("ctx", "head"),
            P("ctx", "head"),
            P("ctx", "head"),
            P("ctx", "head"),
            P(),
            P(),
            P(),
            P("head"),
            P(None, "head"),
        ),
        out_specs=(P("ctx", "head"), P("ctx", "head"), P("ctx", "head")),
        check_vma=False,
    )
```
